32 devices in a mesh: dp: 8 (over z, x), fsdp: 4 (over y, core).
Axes of the slice: x: 2, y: 2, z: 4, core: 2. Of those that a mesh axis runs over, the one named last changes fastest.
Arguments:
- projection_input: bfloat16 [4096, 7168], P(('dp', 'fsdp')), may hold values from -6 to 6
- value_cotangent: bfloat16 [4096, 512], P(('dp', 'fsdp')), may hold values from -6 to 6
- value_weight: bfloat16 [7168, 512], P('fsdp'), may hold values from -0.0625 to 0.0625
- adapter_down_table: bfloat16 [40, 16, 7168], P('dp', None, 'fsdp'), may hold values from -0.0625 to 0.0625
- adapter_up_table: bfloat16 [40, 16, 512], P('dp', None, 'fsdp'), may hold values from -0.25 to 0.25
- adapter_per_block: int32 [32], replicated, may hold values from 0 to 39, as said below
- adapter_table_row: int32 [40], replicated, may hold values from 0 to 39, as said below
Outputs:
- grad_input: bfloat16 [4096, 7168], P(('dp', 'fsdp'))
- grad_down: float32 [40, 16, 7168], P('dp', None, 'fsdp')
- grad_up: float32 [40, 16, 512], P('dp', None, 'fsdp')
The draws below stay inside these ranges and needn't reach their ends.
Inputs may be any that keep to these rules, and one draw needn't show every extreme that they name: adapter_table_row is a permutation: adapter a's factors are row adapter_table_row[a] of the tables, and row r lies on index r // 5 of dp. `adapter_per_block`: among the 4 blocks of one index of dp, all blocks whose adapters lie on the same index of dp name the same adapter.
All inputs are finite; a program needn't handle non-finite values.
Results may differ from the reference program's by a relative error of at most 0.0032.
Values may be sent and summed in bfloat16 or wider, within the bound.
No kernel may reach another device: no remote copies, remote signals or barrier semaphores. Data moves between devices by JAX's collectives and lax.ppermute only.
A program may use at most 64 MiB of HBM per device.

```python
import jax
import jax.numpy as jnp
from jax import lax

INPUT_FEATURES = 7168
VALUE_FEATURES = 512
ADAPTER_RANK = 16
BLOCK = 128
SLOTS = 5
GROUP_BLK = 4
NBLK = 32
TOKENS = 4096
ADAPTER_COUNT = 40
N_DP = 8


def table_order(key):
    return jax.random.permutation(jax.random.fold_in(key, 17), ADAPTER_COUNT).astype(jnp.int32)


def draw_adapter_table_row(key, part):
    return table_order(key)


def draw_adapter_per_block(key, part):
    placement_order = table_order(key)
    key = jax.random.fold_in(key, 2)
    key_first, key_second, key_hot, key_slot = jax.random.split(key, 4)
    first_rank = jax.random.randint(key_first, (N_DP, GROUP_BLK), 0, N_DP)
    second_rank = jax.random.randint(key_second, (N_DP, GROUP_BLK), 0, N_DP)
    hot_order = jax.random.permutation(key_hot, N_DP).astype(jnp.int32)
    owners = hot_order[jnp.minimum(first_rank, second_rank)]
    slot_choose = jax.random.randint(key_slot, (N_DP, N_DP), 0, SLOTS).astype(jnp.int32)
    local_slot = jnp.take_along_axis(slot_choose, owners, axis=1)
    table_rows = owners * SLOTS + local_slot
    inverse = jnp.argsort(placement_order, stable=True).astype(jnp.int32)
    return inverse[table_rows].reshape(NBLK).astype(jnp.int32)


def level_of(stream_key, dims, shards, smallest, high):
    factor_of = 1.0
    for position, parts in shards:
        heights = jax.random.uniform(jax.random.fold_in(jax.random.fold_in(stream_key, 6), position), (parts,), jnp.float32, smallest / len(shards), high / len(shards))
        factor_of = factor_of * jnp.repeat(jnp.exp(heights), dims[position] // parts).reshape((-1,) + (1,) * (len(dims) - 1 - position))
    return factor_of


def centred(key, extent, spread, reach, cuts=(), kind=jnp.bfloat16):
    gain = level_of(key, extent, cuts, -0.22, 0.18) if cuts else 1.0
    array = jax.random.normal(key, extent, jnp.float32) * spread * gain
    return jnp.minimum(jnp.maximum(array, -reach), reach).astype(kind)


def setup_inputs(seed: int = 0) -> dict:
    key_list = jax.random.split(jax.random.key(seed), 8)
    return {
        "projection_input": centred(key_list[0], (TOKENS, INPUT_FEATURES), 1.0, 6.0, ((0, 32),)),
        "value_cotangent": centred(key_list[1], (TOKENS, VALUE_FEATURES), 1.0, 6.0, ((0, 32),)),
        "value_weight": centred(key_list[2], (INPUT_FEATURES, VALUE_FEATURES), INPUT_FEATURES ** -0.5, 0.0625, ((0, 4),)),
        "adapter_down_table": centred(key_list[3], (ADAPTER_COUNT, ADAPTER_RANK, INPUT_FEATURES), INPUT_FEATURES ** -0.5, 0.0625, ((0, 8), (2, 4))),
        "adapter_up_table": centred(key_list[4], (ADAPTER_COUNT, ADAPTER_RANK, VALUE_FEATURES), VALUE_FEATURES ** -0.5, 0.25, ((0, 8), (2, 4))),
        "adapter_per_block": draw_adapter_per_block(jax.random.fold_in(key_list[7], 71), 0),
        "adapter_table_row": draw_adapter_table_row(jax.random.fold_in(key_list[7], 71), 0),
    }


adapter_scale = 2.0


def reference(projection_input, value_cotangent, value_weight, adapter_down_table, adapter_up_table, adapter_per_block, adapter_table_row):
    table_row = adapter_table_row[adapter_per_block].astype(jnp.int32)
    block_total = adapter_per_block.shape[0]
    x_blocks = projection_input.reshape(block_total, BLOCK, INPUT_FEATURES)
    dy_blocks = value_cotangent.reshape(block_total, BLOCK, VALUE_FEATURES)

    def one_block(block_items):
        x_rows, output_grad_rows, row_position = block_items
        down_factor_batch = adapter_down_table[row_position]
        up_factor_batch = adapter_up_table[row_position]
        rank_activations = jnp.dot(x_rows, down_factor_batch.T, preferred_element_type=jnp.float32).astype(jnp.bfloat16)
        rank_backward = (adapter_scale * jnp.dot(output_grad_rows, up_factor_batch.T, preferred_element_type=jnp.float32)).astype(jnp.bfloat16)
        frozen = jnp.dot(output_grad_rows, value_weight.T, preferred_element_type=jnp.float32)
        adapted = jnp.dot(rank_backward, down_factor_batch, preferred_element_type=jnp.float32)
        grad_rows = (frozen + adapted).astype(jnp.bfloat16)
        block_down = jnp.dot(rank_backward.T, x_rows, preferred_element_type=jnp.float32)
        up_for_block = adapter_scale * jnp.dot(rank_activations.T, output_grad_rows, preferred_element_type=jnp.float32)
        return grad_rows, block_down, up_for_block

    grad_rows, block_down, up_for_block = lax.map(one_block, (x_blocks, dy_blocks, table_row))
    counts = jax.ops.segment_sum(jnp.ones_like(table_row), table_row, num_segments=ADAPTER_COUNT)
    divisor = jnp.maximum(counts, 1).astype(jnp.float32)
    grad_down = jax.ops.segment_sum(block_down, table_row, num_segments=ADAPTER_COUNT) / divisor[:, None, None]
    grad_up = jax.ops.segment_sum(up_for_block, table_row, num_segments=ADAPTER_COUNT) / divisor[:, None, None]
    return (grad_rows.reshape(TOKENS, INPUT_FEATURES), grad_down, grad_up)
```

```python
import functools

import jax
import jax.numpy as jnp
from jax import lax
from jax.experimental import pallas as pl
from jax.experimental.pallas import tpu as pltpu
from jax.sharding import PartitionSpec as P

BLOCK = 128
LANES = 128
adapter_scale = 2.0

SMEM = pl.BlockSpec(memory_space=pltpu.SMEM)
VMEM = pl.BlockSpec(memory_space=pltpu.VMEM)
NT = (((1,), (1,)), ((), ()))


def round_up(n):
    return -(-n // LANES) * LANES


def dot(a, b, dims=(((1,), (0,)), ((), ()))):
    return lax.dot_general(a, b, dims, preferred_element_type=jnp.float32)


def pick_kernel(group_blocks, me_ref, apb_ref, row_ref, down_ref, up_ref, send_ref, want_ref, count_ref):
    slots, _, down_part = down_ref.shape
    up_part = up_ref.shape[2]
    up_at = round_up(down_part)
    groups = send_ref.shape[0]
    first = me_ref[0] * slots
    for s in range(slots):
        count_ref[s] = 0

    def group(g, carry):
        want_ref[g] = 0
        for j in range(group_blocks):
            local = row_ref[apb_ref[g * group_blocks + j]] - first

            @pl.when((local >= 0) & (local < slots))
            def _():
                want_ref[g] = local
                count_ref[local] = count_ref[local] + 1

        slot = want_ref[g]
        send_ref[g, :, :down_part] = down_ref[slot]
        send_ref[g, :, up_at : up_at + up_part] = up_ref[slot]
        return carry

    lax.fori_loop(0, groups, group, 0)


def share_kernel(slots, me_ref, apb_ref, row_ref, got_ref, out_ref):
    blocks = out_ref.shape[0]
    for j in range(blocks):
        owner = lax.div(row_ref[apb_ref[me_ref[0] * blocks + j]], slots)
        out_ref[j] = got_ref[owner]


def block_kernel(down_part, up_part, x_ref, dy_ref, fac_ref, grads_ref, back_ref):
    shares = fac_ref.shape[0]
    up_at = round_up(down_part)
    low_t = jnp.zeros((fac_ref.shape[1], BLOCK), jnp.float32)
    back_t = jnp.zeros((fac_ref.shape[1], BLOCK), jnp.float32)
    for k in range(shares):
        back_t += dot(
            fac_ref[k, :, up_at : up_at + up_part],
            dy_ref[:, k * up_part : (k + 1) * up_part],
            NT,
        )
        low_t += dot(
            fac_ref[k, :, :down_part], x_ref[:, k * down_part : (k + 1) * down_part], NT
        )
    low = low_t.astype(jnp.bfloat16)
    scaled = adapter_scale * back_t
    back = scaled.astype(jnp.bfloat16)
    back_ref[...] = scaled.T.astype(jnp.bfloat16)
    for k in range(shares):
        grads_ref[k, :, :down_part] = dot(
            back, x_ref[:, k * down_part : (k + 1) * down_part]
        ).astype(jnp.bfloat16)
        grads_ref[k, :, up_at : up_at + up_part] = (
            adapter_scale * dot(low, dy_ref[:, k * up_part : (k + 1) * up_part])
        ).astype(jnp.bfloat16)


def owner_kernel(slots, me_ref, apb_ref, row_ref, got_ref, out_ref, acc_ref):
    blocks = got_ref.shape[0]
    acc_ref[...] = jnp.zeros_like(acc_ref)
    for j in range(blocks):
        owner = lax.div(row_ref[apb_ref[me_ref[0] * blocks + j]], slots)
        acc_ref[owner] += got_ref[j].astype(jnp.float32)
    out_ref[...] = acc_ref[...].astype(jnp.bfloat16)


def total_kernel(want_ref, count_ref, got_ref, down_ref, up_ref):
    slots, _, down_part = down_ref.shape
    up_part = up_ref.shape[2]
    up_at = round_up(down_part)
    down_ref[...] = jnp.zeros_like(down_ref)
    up_ref[...] = jnp.zeros_like(up_ref)

    def group(g, carry):
        slot = want_ref[g]
        down_ref[slot] += got_ref[g, :, :down_part].astype(jnp.float32)
        up_ref[slot] += got_ref[g, :, up_at : up_at + up_part].astype(jnp.float32)
        return carry

    lax.fori_loop(0, got_ref.shape[0], group, 0)
    for s in range(slots):
        divisor = jnp.maximum(count_ref[s], 1).astype(jnp.float32)
        down_ref[s] = down_ref[s] / divisor
        up_ref[s] = up_ref[s] / divisor


def input_kernel(half, *refs):
    place_ref, dy_ref, back_ref, fac_ref = refs[:4]
    weights = refs[4:8]
    out_ref, buf, sems = refs[-3:]
    k = pl.program_id(0)
    rows = buf.shape[1]
    copies = [pltpu.make_async_copy(weights[i], buf.at[i], sems.at[i]) for i in range(4)]
    for i in range(4):

        @pl.when(k == 0)
        def _():
            copies[i].start()

    for i in range(4):

        @pl.when(k == i)
        def _():
            copies[i].wait()

    out_ref[...] = (
        dot(dy_ref[...], buf[k], NT)
        + dot(back_ref[...], fac_ref[place_ref[k], :, half * rows : (half + 1) * rows])
    ).astype(jnp.bfloat16)


def input_half(half, place, dy, back, factors, weights, out, width):
    rows, features = weights[0].shape
    operands = [dy, back, factors, *weights]
    whole = [
        pl.BlockSpec(a.shape, functools.partial(lambda n, *_: (0,) * n, a.ndim))
        for a in operands[:3]
    ]
    specs = whole + [pl.BlockSpec(memory_space=pl.ANY)] * 4
    aliases = {}
    if out is not None:
        operands.append(out)
        specs.append(pl.BlockSpec(memory_space=pl.ANY))
        aliases = {len(operands): 0}
    return pl.pallas_call(
        functools.partial(input_kernel, half),
        grid_spec=pltpu.PrefetchScalarGridSpec(
            num_scalar_prefetch=1,
            grid=(4,),
            in_specs=specs,
            out_specs=pl.BlockSpec((dy.shape[0], rows), lambda k, place: (0, 2 * place[k] + half)),
            scratch_shapes=[
                pltpu.VMEM((4, rows, features), jnp.bfloat16),
                pltpu.SemaphoreType.DMA((4,)),
            ],
        ),
        out_shape=jax.ShapeDtypeStruct((dy.shape[0], width), jnp.bfloat16),
        input_output_aliases=aliases,
        compiler_params=pltpu.CompilerParams(vmem_limit_bytes=32 << 20),
        cost_estimate=pl.CostEstimate(
            flops=8 * dy.shape[0] * rows * features,
            bytes_accessed=8 * rows * features + 8 * dy.shape[0] * rows,
            transcendentals=0,
        ),
    )(place, *operands)


def call(kernel, out_shape, out_specs, *operands, smem=0, scratch=()):
    return pl.pallas_call(
        kernel,
        out_shape=out_shape,
        in_specs=[SMEM] * smem + [VMEM] * (len(operands) - smem),
        out_specs=out_specs,
        scratch_shapes=scratch,
        compiler_params=pltpu.CompilerParams(vmem_limit_bytes=32 << 20),
    )(*operands)


def per_device(
    projection_input,
    value_cotangent,
    value_weight,
    adapter_down_table,
    adapter_up_table,
    adapter_per_block,
    adapter_table_row,
):
    dp_count = lax.axis_size("dp")
    fsdp_count = lax.axis_size("fsdp")
    me = lax.axis_index("dp").reshape(1)
    at = lax.axis_index("fsdp")
    tok_rows, width = projection_input.shape
    slots, rank, down_part = adapter_down_table.shape
    up_part = adapter_up_table.shape[2]
    assert tok_rows == BLOCK
    wide = round_up(down_part) + round_up(up_part)
    bf16 = jnp.bfloat16

    def shaped(*shape, dtype=bf16):
        return jax.ShapeDtypeStruct(shape, dtype)

    by_permute = fsdp_count == 4 and value_weight.shape[0] % 256 == 0

    def cross(array, bit):
        return lax.ppermute(array, "fsdp", [(i, i ^ bit) for i in range(fsdp_count)])

    half_rows = value_weight.shape[0] // 2
    halves = [value_weight[:half_rows], value_weight[half_rows:]]

    def gather_half(own):
        far = cross(own, 2)
        return own, cross(own, 1), far, cross(far, 1)

    index = (me, adapter_per_block, adapter_table_row)
    send, want, count = call(
        functools.partial(pick_kernel, fsdp_count),
        (
            shaped(dp_count, rank, wide),
            shaped(dp_count, dtype=jnp.int32),
            shaped(slots, dtype=jnp.int32),
        ),
        (VMEM, SMEM, SMEM),
        *index,
        adapter_down_table,
        adapter_up_table,
        smem=3,
    )
    if by_permute:
        first = gather_half(halves[0])
    owned = lax.all_to_all(send, "dp", split_axis=0, concat_axis=0, tiled=True)
    share = call(
        functools.partial(share_kernel, slots),
        shaped(fsdp_count, rank, wide),
        VMEM,
        *index,
        owned,
        smem=3,
    )
    factors = lax.all_to_all(share, "fsdp", split_axis=0, concat_axis=0, tiled=True)
    grads, back = call(
        functools.partial(block_kernel, down_part, up_part),
        (shaped(fsdp_count, rank, wide), shaped(BLOCK, rank)),
        (VMEM, VMEM),
        projection_input,
        value_cotangent,
        factors,
    )
    got = lax.all_to_all(grads, "fsdp", split_axis=0, concat_axis=0, tiled=True)
    if by_permute:
        second_own, got = lax.optimization_barrier((halves[1], got))
        second = gather_half(second_own)
    sums = call(
        functools.partial(owner_kernel, slots),
        shaped(dp_count, rank, wide),
        VMEM,
        *index,
        got,
        smem=3,
        scratch=[pltpu.VMEM((dp_count, rank, wide), jnp.float32)],
    )
    arrived = lax.all_to_all(sums, "dp", split_axis=0, concat_axis=0, tiled=True)
    grad_down, grad_up = call(
        total_kernel,
        (
            shaped(slots, rank, down_part, dtype=jnp.float32),
            shaped(slots, rank, up_part, dtype=jnp.float32),
        ),
        (VMEM, VMEM),
        want,
        count,
        arrived,
        smem=2,
    )
    if by_permute:
        place = at ^ jnp.arange(4, dtype=jnp.int32)
        grad_input = None
        for half, weights in enumerate((first, second)):
            grad_input = input_half(
                half, place, value_cotangent, back, factors, weights, grad_input, width
            )
    else:
        weight = lax.all_gather(value_weight, "fsdp", axis=0, tiled=True)
        adapter_term = jnp.einsum(
            "tr,krd->tkd", back, factors[:, :, :down_part], preferred_element_type=jnp.float32
        )
        frozen_term = jnp.einsum(
            "tc,dc->td", value_cotangent, weight, preferred_element_type=jnp.float32
        )
        grad_input = (frozen_term + adapter_term.reshape(tok_rows, width)).astype(bf16)
    return (grad_input, grad_down, grad_up)


def solution(mesh):
    return jax.shard_map(
        per_device,
        mesh=mesh,
        in_specs=(
            P(("dp", "fsdp"), None),
            P(("dp", "fsdp"), None),
            P("fsdp", None),
            P("dp", None, "fsdp"),
            P("dp", None, "fsdp"),
            P(),
            P(),
        ),
        out_specs=(P(("dp", "fsdp"), None), P("dp", None, "fsdp"), P("dp", None, "fsdp")),
        check_vma=False,
    )
```

```python
import functools

import jax
import jax.numpy as jnp
from jax import lax
from jax.experimental import pallas as pl
from jax.experimental.pallas import tpu as pltpu
from jax.sharding import PartitionSpec as P

BLOCK = 128
LANES = 128
adapter_scale = 2.0

SMEM = pl.BlockSpec(memory_space=pltpu.SMEM)
VMEM = pl.BlockSpec(memory_space=pltpu.VMEM)
NT = (((1,), (1,)), ((), ()))


def round_up(n):
    return -(-n // LANES) * LANES


def dot(a, b, dims=(((1,), (0,)), ((), ()))):
    return lax.dot_general(a, b, dims, preferred_element_type=jnp.float32)


def pick_kernel(group_blocks, me_ref, apb_ref, row_ref, down_ref, up_ref, send_ref, want_ref, count_ref):
    slots, _, down_part = down_ref.shape
    up_part = up_ref.shape[2]
    up_at = round_up(down_part)
    groups = send_ref.shape[0]
    first = me_ref[0] * slots
    for s in range(slots):
        count_ref[s] = 0

    def group(g, carry):
        want_ref[g] = 0
        for j in range(group_blocks):
            local = row_ref[apb_ref[g * group_blocks + j]] - first

            @pl.when((local >= 0) & (local < slots))
            def _():
                want_ref[g] = local
                count_ref[local] = count_ref[local] + 1

        slot = want_ref[g]
        send_ref[g, :, :down_part] = down_ref[slot]
        send_ref[g, :, up_at : up_at + up_part] = up_ref[slot]
        return carry

    lax.fori_loop(0, groups, group, 0)


def share_kernel(slots, me_ref, apb_ref, row_ref, got_ref, out_ref):
    blocks = out_ref.shape[0]
    for j in range(blocks):
        owner = lax.div(row_ref[apb_ref[me_ref[0] * blocks + j]], slots)
        out_ref[j] = got_ref[owner]


def block_kernel(down_part, up_part, x_ref, dy_ref, fac_ref, grads_ref, back_ref, dy_t_ref):
    shares = fac_ref.shape[0]
    up_at = round_up(down_part)
    low_t = jnp.zeros((fac_ref.shape[1], BLOCK), jnp.float32)
    back_t = jnp.zeros((fac_ref.shape[1], BLOCK), jnp.float32)
    for k in range(shares):
        back_t += dot(
            fac_ref[k, :, up_at : up_at + up_part],
            dy_ref[:, k * up_part : (k + 1) * up_part],
            NT,
        )
        low_t += dot(
            fac_ref[k, :, :down_part], x_ref[:, k * down_part : (k + 1) * down_part], NT
        )
    low = low_t.astype(jnp.bfloat16)
    scaled = adapter_scale * back_t
    back = scaled.astype(jnp.bfloat16)
    back_ref[...] = scaled.T.astype(jnp.bfloat16)
    dy_t_ref[...] = dy_ref[...].astype(jnp.float32).T.astype(jnp.bfloat16)
    for k in range(shares):
        grads_ref[k, :, :down_part] = dot(
            back, x_ref[:, k * down_part : (k + 1) * down_part]
        ).astype(jnp.bfloat16)
        grads_ref[k, :, up_at : up_at + up_part] = (
            adapter_scale * dot(low, dy_ref[:, k * up_part : (k + 1) * up_part])
        ).astype(jnp.bfloat16)


def owner_kernel(slots, me_ref, apb_ref, row_ref, got_ref, out_ref, acc_ref):
    blocks = got_ref.shape[0]
    acc_ref[...] = jnp.zeros_like(acc_ref)
    for j in range(blocks):
        owner = lax.div(row_ref[apb_ref[me_ref[0] * blocks + j]], slots)
        acc_ref[owner] += got_ref[j].astype(jnp.float32)
    out_ref[...] = acc_ref[...].astype(jnp.bfloat16)


def total_kernel(want_ref, count_ref, got_ref, down_ref, up_ref):
    slots, _, down_part = down_ref.shape
    up_part = up_ref.shape[2]
    up_at = round_up(down_part)
    down_ref[...] = jnp.zeros_like(down_ref)
    up_ref[...] = jnp.zeros_like(up_ref)

    def group(g, carry):
        slot = want_ref[g]
        down_ref[slot] += got_ref[g, :, :down_part].astype(jnp.float32)
        up_ref[slot] += got_ref[g, :, up_at : up_at + up_part].astype(jnp.float32)
        return carry

    lax.fori_loop(0, got_ref.shape[0], group, 0)
    for s in range(slots):
        divisor = jnp.maximum(count_ref[s], 1).astype(jnp.float32)
        down_ref[s] = down_ref[s] / divisor
        up_ref[s] = up_ref[s] / divisor


def input_kernel(half, *refs):
    place_ref, dy_ref, back_ref, fac_ref = refs[:4]
    weights = refs[4:8]
    out_ref, buf, sems = refs[-3:]
    k = pl.program_id(0)
    rows = buf.shape[1]
    copies = [pltpu.make_async_copy(weights[i], buf.at[i], sems.at[i]) for i in range(4)]
    for i in range(4):

        @pl.when(k == 0)
        def _():
            copies[i].start()

    for i in range(4):

        @pl.when(k == i)
        def _():
            copies[i].wait()

    frozen_t = dot(buf[k], dy_ref[...])
    out_ref[...] = (
        frozen_t.T
        + dot(back_ref[...], fac_ref[place_ref[k], :, half * rows : (half + 1) * rows])
    ).astype(jnp.bfloat16)


def input_half(half, place, dy_t, back, factors, weights, out, width):
    rows, features = weights[0].shape
    tokens = dy_t.shape[1]
    operands = [dy_t, back, factors, *weights]
    whole = [
        pl.BlockSpec(a.shape, functools.partial(lambda n, *_: (0,) * n, a.ndim))
        for a in operands[:3]
    ]
    specs = whole + [pl.BlockSpec(memory_space=pl.ANY)] * 4
    aliases = {}
    if out is not None:
        operands.append(out)
        specs.append(pl.BlockSpec(memory_space=pl.ANY))
        aliases = {len(operands): 0}
    return pl.pallas_call(
        functools.partial(input_kernel, half),
        grid_spec=pltpu.PrefetchScalarGridSpec(
            num_scalar_prefetch=1,
            grid=(4,),
            in_specs=specs,
            out_specs=pl.BlockSpec((tokens, rows), lambda k, place: (0, 2 * place[k] + half)),
            scratch_shapes=[
                pltpu.VMEM((4, rows, features), jnp.bfloat16),
                pltpu.SemaphoreType.DMA((4,)),
            ],
        ),
        out_shape=jax.ShapeDtypeStruct((tokens, width), jnp.bfloat16),
        input_output_aliases=aliases,
        compiler_params=pltpu.CompilerParams(vmem_limit_bytes=32 << 20),
        cost_estimate=pl.CostEstimate(
            flops=8 * tokens * rows * features,
            bytes_accessed=8 * rows * features + 8 * tokens * rows,
            transcendentals=0,
        ),
    )(place, *operands)


def call(kernel, out_shape, out_specs, *operands, smem=0, scratch=(), vmem=32):
    return pl.pallas_call(
        kernel,
        out_shape=out_shape,
        in_specs=[SMEM] * smem + [VMEM] * (len(operands) - smem),
        out_specs=out_specs,
        scratch_shapes=scratch,
        compiler_params=pltpu.CompilerParams(vmem_limit_bytes=vmem << 20),
    )(*operands)


def per_device(
    projection_input,
    value_cotangent,
    value_weight,
    adapter_down_table,
    adapter_up_table,
    adapter_per_block,
    adapter_table_row,
):
    dp_count = lax.axis_size("dp")
    fsdp_count = lax.axis_size("fsdp")
    me = lax.axis_index("dp").reshape(1)
    at = lax.axis_index("fsdp")
    tok_rows, width = projection_input.shape
    slots, rank, down_part = adapter_down_table.shape
    up_part = adapter_up_table.shape[2]
    assert tok_rows == BLOCK
    wide = round_up(down_part) + round_up(up_part)
    bf16 = jnp.bfloat16

    def shaped(*shape, dtype=bf16):
        return jax.ShapeDtypeStruct(shape, dtype)

    by_permute = fsdp_count == 4 and value_weight.shape[0] % 256 == 0

    def cross(array, bit):
        return lax.ppermute(array, "fsdp", [(i, i ^ bit) for i in range(fsdp_count)])

    half_rows = value_weight.shape[0] // 2

    index = (me, adapter_per_block, adapter_table_row)
    send, want, count = call(
        functools.partial(pick_kernel, fsdp_count),
        (
            shaped(dp_count, rank, wide),
            shaped(dp_count, dtype=jnp.int32),
            shaped(slots, dtype=jnp.int32),
        ),
        (VMEM, SMEM, SMEM),
        *index,
        adapter_down_table,
        adapter_up_table,
        smem=3,
        vmem=60,
    )
    if by_permute:
        value_weight, send = lax.optimization_barrier((value_weight, send))
    halves = [value_weight[:half_rows], value_weight[half_rows:]]
    owned = lax.all_to_all(send, "dp", split_axis=0, concat_axis=0, tiled=True)
    if by_permute:
        far = cross(halves[0], 2)
        owned, far = lax.optimization_barrier((owned, far))
        first = halves[0], cross(halves[0], 1), far, cross(far, 1)
    share = call(
        functools.partial(share_kernel, slots),
        shaped(fsdp_count, rank, wide),
        VMEM,
        *index,
        owned,
        smem=3,
    )
    factors = lax.all_to_all(share, "fsdp", split_axis=0, concat_axis=0, tiled=True)
    if by_permute:
        factors, first = lax.optimization_barrier((factors, first))
    grads, back, dy_t = call(
        functools.partial(block_kernel, down_part, up_part),
        (
            shaped(fsdp_count, rank, wide),
            shaped(BLOCK, rank),
            shaped(value_cotangent.shape[1], BLOCK),
        ),
        (VMEM, VMEM, VMEM),
        projection_input,
        value_cotangent,
        factors,
    )
    got = lax.all_to_all(grads, "fsdp", split_axis=0, concat_axis=0, tiled=True)
    sums = call(
        functools.partial(owner_kernel, slots),
        shaped(dp_count, rank, wide),
        VMEM,
        *index,
        got,
        smem=3,
        scratch=[pltpu.VMEM((dp_count, rank, wide), jnp.float32)],
    )
    if by_permute:
        own, sums = lax.optimization_barrier((halves[1], sums))
        far = cross(own, 2)
    arrived = lax.all_to_all(sums, "dp", split_axis=0, concat_axis=0, tiled=True)
    if by_permute:
        place = at ^ jnp.arange(4, dtype=jnp.int32)
        grad_input = input_half(0, place, dy_t, back, factors, first, None, width)
        arrived, far, grad_input = lax.optimization_barrier((arrived, far, grad_input))
        second = own, cross(own, 1), far, cross(far, 1)
    grad_down, grad_up = call(
        total_kernel,
        (
            shaped(slots, rank, down_part, dtype=jnp.float32),
            shaped(slots, rank, up_part, dtype=jnp.float32),
        ),
        (VMEM, VMEM),
        want,
        count,
        arrived,
        smem=2,
    )
    if by_permute:
        grad_input = input_half(1, place, dy_t, back, factors, second, grad_input, width)
    else:
        weight = lax.all_gather(value_weight, "fsdp", axis=0, tiled=True)
        adapter_term = jnp.einsum(
            "tr,krd->tkd", back, factors[:, :, :down_part], preferred_element_type=jnp.float32
        )
        frozen_term = jnp.einsum(
            "tc,dc->td", value_cotangent, weight, preferred_element_type=jnp.float32
        )
        grad_input = (frozen_term + adapter_term.reshape(tok_rows, width)).astype(bf16)
    return (grad_input, grad_down, grad_up)


def solution(mesh):
    return jax.shard_map(
        per_device,
        mesh=mesh,
        in_specs=(
            P(("dp", "fsdp"), None),
            P(("dp", "fsdp"), None),
            P("fsdp", None),
            P("dp", None, "fsdp"),
            P("dp", None, "fsdp"),
            P(),
            P(),
        ),
        out_specs=(P(("dp", "fsdp"), None), P("dp", None, "fsdp"), P("dp", None, "fsdp")),
        check_vma=False,
    )
```

```python
import functools

import jax
import jax.numpy as jnp
from jax import lax
from jax.experimental import pallas as pl
from jax.experimental.pallas import tpu as pltpu
from jax.sharding import PartitionSpec as P

BLOCK = 128
LANES = 128
adapter_scale = 2.0

SMEM = pl.BlockSpec(memory_space=pltpu.SMEM)
VMEM = pl.BlockSpec(memory_space=pltpu.VMEM)
NT = (((1,), (1,)), ((), ()))


def round_up(n):
    return -(-n // LANES) * LANES


def dot(a, b, dims=(((1,), (0,)), ((), ()))):
    return lax.dot_general(a, b, dims, preferred_element_type=jnp.float32)


def turned(a):
    return a.astype(jnp.float32).T.astype(a.dtype)


def pick_kernel(group_blocks, me_ref, apb_ref, row_ref, down_ref, up_ref, send_ref, want_ref, count_ref):
    slots, _, down_part = down_ref.shape
    up_part = up_ref.shape[2]
    up_at = round_up(down_part)
    groups = send_ref.shape[0]
    first = me_ref[0] * slots
    for s in range(slots):
        count_ref[s] = 0

    def group(g, carry):
        want_ref[g] = 0
        for j in range(group_blocks):
            local = row_ref[apb_ref[g * group_blocks + j]] - first

            @pl.when((local >= 0) & (local < slots))
            def _():
                want_ref[g] = local
                count_ref[local] = count_ref[local] + 1

        slot = want_ref[g]
        send_ref[g, :, :down_part] = down_ref[slot]
        send_ref[g, :, up_at : up_at + up_part] = up_ref[slot]
        return carry

    lax.fori_loop(0, groups, group, 0)


def share_kernel(slots, me_ref, apb_ref, row_ref, got_ref, out_ref):
    blocks = out_ref.shape[0]
    for j in range(blocks):
        owner = lax.div(row_ref[apb_ref[me_ref[0] * blocks + j]], slots)
        out_ref[j] = got_ref[owner]


def block_kernel(
    down_part, up_part, x_ref, dy_ref, fac_ref, grads_ref, back_ref, dy_t_ref, x_buf, sems
):
    shares = fac_ref.shape[0]
    up_at = round_up(down_part)
    back_at = up_at + round_up(up_part)
    parts = shares if down_part % LANES == 0 else 1
    copies = []
    for k in range(parts):
        columns = pl.ds(k * (x_ref.shape[1] // parts), x_ref.shape[1] // parts)
        copies.append(
            pltpu.make_async_copy(x_ref.at[:, columns], x_buf.at[:, columns], sems.at[k])
        )
        copies[k].start()
    low_t = jnp.zeros((fac_ref.shape[1], BLOCK), jnp.float32)
    back_t = jnp.zeros((fac_ref.shape[1], BLOCK), jnp.float32)
    for k in range(shares):
        back_t += dot(
            fac_ref[k, :, up_at : up_at + up_part],
            dy_ref[:, k * up_part : (k + 1) * up_part],
            NT,
        )
    scaled = adapter_scale * back_t
    back = scaled.astype(jnp.bfloat16)
    back_ref[...] = scaled.T.astype(jnp.bfloat16)
    dy_t_ref[...] = turned(dy_ref[...])
    for k in range(shares):
        if k < parts:
            copies[k].wait()
        x = x_buf[:, k * down_part : (k + 1) * down_part]
        low_t += dot(fac_ref[k, :, :down_part], x, NT)
        grads_ref[k, :, :down_part] = dot(back, x).astype(jnp.bfloat16)
        grads_ref[k, :, back_at:] = back
    low = low_t.astype(jnp.bfloat16)
    for k in range(shares):
        grads_ref[k, :, up_at : up_at + up_part] = (
            adapter_scale * dot(low, dy_ref[:, k * up_part : (k + 1) * up_part])
        ).astype(jnp.bfloat16)


def owner_kernel(slots, me_ref, apb_ref, row_ref, got_ref, out_ref, acc_ref):
    blocks = got_ref.shape[0]
    acc_ref[...] = jnp.zeros_like(acc_ref)
    for j in range(blocks):
        owner = lax.div(row_ref[apb_ref[me_ref[0] * blocks + j]], slots)
        acc_ref[owner] += got_ref[j, :, : acc_ref.shape[2]].astype(jnp.float32)
    out_ref[...] = acc_ref[...].astype(jnp.bfloat16)


def total_kernel(want_ref, count_ref, got_ref, down_ref, up_ref):
    slots, _, down_part = down_ref.shape
    up_part = up_ref.shape[2]
    up_at = round_up(down_part)
    down_ref[...] = jnp.zeros_like(down_ref)
    up_ref[...] = jnp.zeros_like(up_ref)

    def group(g, carry):
        slot = want_ref[g]
        down_ref[slot] += got_ref[g, :, :down_part].astype(jnp.float32)
        up_ref[slot] += got_ref[g, :, up_at : up_at + up_part].astype(jnp.float32)
        return carry

    lax.fori_loop(0, got_ref.shape[0], group, 0)
    for s in range(slots):
        divisor = jnp.maximum(count_ref[s], 1).astype(jnp.float32)
        down_ref[s] = down_ref[s] / divisor
        up_ref[s] = up_ref[s] / divisor


def far_kernel(at_ref, w_ref, dy2_ref, dy3_ref, share_ref, got_ref, z2_ref, z3_ref):
    rows = z2_ref.shape[1]
    tokens = dy2_ref.shape[0]
    start = w_ref.shape[0] - rows
    dy_t = jnp.concatenate([turned(dy2_ref[...]), turned(dy3_ref[...])], axis=1)
    frozen_t = dot(w_ref[start:, :], dy_t)
    for i, z_ref in enumerate((z2_ref, z3_ref)):
        peer = lax.bitwise_xor(at_ref[0], 2 + i)
        back = turned(got_ref[peer, :, got_ref.shape[2] - tokens :])
        z_ref[...] = (
            frozen_t[:, i * tokens : (i + 1) * tokens].T
            + dot(back, share_ref[peer, :, start : w_ref.shape[0]])
        ).astype(jnp.bfloat16)


def input_kernel(
    at_ref, dy_t_ref, back_ref, fac_ref, w0_ref, w1_ref, w2_ref, w3_ref, out_ref, buf, sems
):
    part = w0_ref.shape[0]
    copies = []
    for k, w_ref in enumerate((w0_ref, w1_ref, w2_ref, w3_ref)):
        rows = w_ref.shape[0]
        peer = lax.bitwise_xor(at_ref[0], k)
        buf[k, :, :rows] = (
            dot(w_ref[...], dy_t_ref[...]).T + dot(back_ref[...], fac_ref[peer, :, :rows])
        ).astype(jnp.bfloat16)
        first = pl.multiple_of(peer * part, LANES)
        copy = pltpu.make_async_copy(
            buf.at[k, :, pl.ds(0, rows)], out_ref.at[:, pl.ds(first, rows)], sems.at[k]
        )
        copy.start()
        copies.append(copy)
    for copy in copies:
        copy.wait()


def place_kernel(at_ref, z2_ref, z3_ref, in_ref, out_ref, sems):
    rows = z2_ref.shape[1]
    part = out_ref.shape[1] // 4
    copies = []
    for i, z_ref in enumerate((z2_ref, z3_ref)):
        peer = lax.bitwise_xor(at_ref[0], 2 + i)
        first = pl.multiple_of(peer * part + (part - rows), LANES)
        copy = pltpu.make_async_copy(z_ref, out_ref.at[:, pl.ds(first, rows)], sems.at[i])
        copy.start()
        copies.append(copy)
    for copy in copies:
        copy.wait()


def call(
    kernel, out_shape, out_specs, *operands, smem=0, scratch=(), vmem=32, specs=None, aliases=None
):
    return pl.pallas_call(
        kernel,
        out_shape=out_shape,
        in_specs=[SMEM] * smem + (specs or [VMEM] * (len(operands) - smem)),
        input_output_aliases=aliases or {},
        out_specs=out_specs,
        scratch_shapes=scratch,
        compiler_params=pltpu.CompilerParams(vmem_limit_bytes=vmem << 20),
    )(*operands)


def per_device(
    projection_input,
    value_cotangent,
    value_weight,
    adapter_down_table,
    adapter_up_table,
    adapter_per_block,
    adapter_table_row,
):
    dp_count = lax.axis_size("dp")
    fsdp_count = lax.axis_size("fsdp")
    me = lax.axis_index("dp").reshape(1)
    at = lax.axis_index("fsdp")
    tok_rows, width = projection_input.shape
    slots, rank, down_part = adapter_down_table.shape
    up_part = adapter_up_table.shape[2]
    assert tok_rows == BLOCK
    wide = round_up(down_part) + round_up(up_part)
    bf16 = jnp.bfloat16

    def shaped(*shape, dtype=bf16):
        return jax.ShapeDtypeStruct(shape, dtype)

    by_permute = fsdp_count == 4 and down_part % 256 == 0
    near_rows = 3 * down_part // 8 // LANES * LANES

    def cross(array, bit):
        return lax.ppermute(array, "fsdp", [(i, i ^ bit) for i in range(fsdp_count)])

    index = (me, adapter_per_block, adapter_table_row)
    send, want, count = call(
        functools.partial(pick_kernel, fsdp_count),
        (
            shaped(dp_count, rank, wide),
            shaped(dp_count, dtype=jnp.int32),
            shaped(slots, dtype=jnp.int32),
        ),
        (VMEM, SMEM, SMEM),
        *index,
        adapter_down_table,
        adapter_up_table,
        smem=3,
        vmem=60,
    )
    if by_permute:
        value_weight, send = lax.optimization_barrier((value_weight, send))
    owned = lax.all_to_all(send, "dp", split_axis=0, concat_axis=0, tiled=True)
    if by_permute:
        far = cross(value_weight[:near_rows], 2)
        dy2 = cross(value_cotangent, 2)
        owned, far, dy2 = lax.optimization_barrier((owned, far, dy2))
        near = cross(value_weight, 1), far, cross(far, 1)
        dys = dy2, cross(dy2, 1)
    share = call(
        functools.partial(share_kernel, slots),
        shaped(fsdp_count, rank, wide),
        VMEM,
        *index,
        owned,
        smem=3,
    )
    factors = lax.all_to_all(share, "fsdp", split_axis=0, concat_axis=0, tiled=True)
    if by_permute:
        factors, near, dys = lax.optimization_barrier((factors, near, dys))
    grads, back, dy_t = call(
        functools.partial(block_kernel, down_part, up_part),
        (
            shaped(fsdp_count, rank, wide + BLOCK),
            shaped(BLOCK, rank),
            shaped(value_cotangent.shape[1], BLOCK),
        ),
        (VMEM, VMEM, VMEM),
        projection_input,
        value_cotangent,
        factors,
        specs=[pl.BlockSpec(memory_space=pl.ANY), VMEM, VMEM],
        scratch=[
            pltpu.VMEM((BLOCK, width), bf16),
            pltpu.SemaphoreType.DMA((fsdp_count,)),
        ],
        vmem=56,
    )
    got = lax.all_to_all(grads, "fsdp", split_axis=0, concat_axis=0, tiled=True)
    sums = call(
        functools.partial(owner_kernel, slots),
        shaped(dp_count, rank, wide),
        VMEM,
        *index,
        got,
        smem=3,
        scratch=[pltpu.VMEM((dp_count, rank, wide), jnp.float32)],
    )
    arrived = lax.all_to_all(sums, "dp", split_axis=0, concat_axis=0, tiled=True)
    if by_permute:
        at = at.reshape(1)
        far_rows = down_part - near_rows
        z2, z3 = call(
            far_kernel,
            (shaped(BLOCK, far_rows), shaped(BLOCK, far_rows)),
            (VMEM, VMEM),
            at,
            value_weight,
            *dys,
            share,
            got,
            smem=1,
        )
        z2, z3 = cross(z2, 2), cross(z3, 3)
        grad_input = call(
            input_kernel,
            shaped(tok_rows, width),
            pl.BlockSpec(memory_space=pl.ANY),
            at,
            dy_t,
            back,
            factors,
            value_weight,
            *near,
            smem=1,
            scratch=[
                pltpu.VMEM((fsdp_count, tok_rows, down_part), bf16),
                pltpu.SemaphoreType.DMA((fsdp_count,)),
            ],
        )
        grad_input = call(
            place_kernel,
            shaped(tok_rows, width),
            pl.BlockSpec(memory_space=pl.ANY),
            at,
            z2,
            z3,
            grad_input,
            smem=1,
            specs=[VMEM, VMEM, pl.BlockSpec(memory_space=pl.ANY)],
            scratch=[pltpu.SemaphoreType.DMA((2,))],
            aliases={3: 0},
        )
        arrived, grad_input = lax.optimization_barrier((arrived, grad_input))
    grad_down, grad_up = call(
        total_kernel,
        (
            shaped(slots, rank, down_part, dtype=jnp.float32),
            shaped(slots, rank, up_part, dtype=jnp.float32),
        ),
        (VMEM, VMEM),
        want,
        count,
        arrived,
        smem=2,
    )
    if not by_permute:
        weight = lax.all_gather(value_weight, "fsdp", axis=0, tiled=True)
        adapter_term = jnp.einsum(
            "tr,krd->tkd", back, factors[:, :, :down_part], preferred_element_type=jnp.float32
        )
        frozen_term = jnp.einsum(
            "tc,dc->td", value_cotangent, weight, preferred_element_type=jnp.float32
        )
        grad_input = (frozen_term + adapter_term.reshape(tok_rows, width)).astype(bf16)
    return (grad_input, grad_down, grad_up)


def solution(mesh):
    return jax.shard_map(
        per_device,
        mesh=mesh,
        in_specs=(
            P(("dp", "fsdp"), None),
            P(("dp", "fsdp"), None),
            P("fsdp", None),
            P("dp", None, "fsdp"),
            P("dp", None, "fsdp"),
            P(),
            P(),
        ),
        out_specs=(P(("dp", "fsdp"), None), P("dp", None, "fsdp"), P("dp", None, "fsdp")),
        check_vma=False,
    )
```

```python
import functools

import jax
import jax.numpy as jnp
from jax import lax
from jax.experimental import pallas as pl
from jax.experimental.pallas import tpu as pltpu
from jax.sharding import PartitionSpec as P

BLOCK = 128
LANES = 128
adapter_scale = 2.0

SMEM = pl.BlockSpec(memory_space=pltpu.SMEM)
VMEM = pl.BlockSpec(memory_space=pltpu.VMEM)
ANY = pl.BlockSpec(memory_space=pl.ANY)
NT = (((1,), (1,)), ((), ()))


def round_up(n):
    return -(-n // LANES) * LANES


def dot(a, b, dims=(((1,), (0,)), ((), ()))):
    return lax.dot_general(a, b, dims, preferred_element_type=jnp.float32)


def turned(a):
    return a.astype(jnp.float32).T.astype(a.dtype)


def fetch(sources, targets, sems):
    copies = [
        pltpu.make_async_copy(source, target, sems.at[i])
        for i, (source, target) in enumerate(zip(sources, targets))
    ]
    for copy in copies:
        copy.start()
    return copies


def copy_kernel(from_ref, to_ref, sem):
    copy = pltpu.make_async_copy(from_ref, to_ref, sem)
    copy.start()
    copy.wait()


def pick_kernel(
    group_blocks, me_ref, apb_hbm, row_hbm, down_hbm, up_hbm, send_ref, want_ref, count_ref,
    apb_ref, row_ref, down_ref, up_ref, sems,
):
    copies = fetch(
        (apb_hbm, row_hbm, down_hbm, up_hbm), (apb_ref, row_ref, down_ref, up_ref), sems
    )
    slots, _, down_part = down_ref.shape
    up_part = up_ref.shape[2]
    up_at = round_up(down_part)
    groups = send_ref.shape[0]
    first = me_ref[0] * slots
    for s in range(slots):
        count_ref[s] = 0
    copies[0].wait()
    copies[1].wait()

    def group(g, carry):
        want_ref[g] = 0
        for j in range(group_blocks):
            local = row_ref[apb_ref[g * group_blocks + j]] - first

            @pl.when((local >= 0) & (local < slots))
            def _():
                want_ref[g] = local
                count_ref[local] = count_ref[local] + 1

        return carry

    lax.fori_loop(0, groups, group, 0)
    copies[2].wait()
    copies[3].wait()

    def put(g, carry):
        slot = want_ref[g]
        send_ref[g, :, :down_part] = down_ref[slot]
        send_ref[g, :, up_at : up_at + up_part] = up_ref[slot]
        return carry

    lax.fori_loop(0, groups, put, 0)


def share_kernel(slots, me_ref, apb_ref, row_ref, got_ref, out_ref):
    blocks = out_ref.shape[0]
    for j in range(blocks):
        owner = lax.div(row_ref[apb_ref[me_ref[0] * blocks + j]], slots)
        out_ref[j] = got_ref[owner]


def block_kernel(
    down_part, up_part, x_ref, dy_ref, fac_ref, grads_ref, back_ref
):
    shares = fac_ref.shape[0]
    up_at = round_up(down_part)
    back_at = up_at + round_up(up_part)
    low_t = jnp.zeros((fac_ref.shape[1], BLOCK), jnp.float32)
    back_t = jnp.zeros((fac_ref.shape[1], BLOCK), jnp.float32)
    for k in range(shares):
        back_t += dot(
            fac_ref[k, :, up_at : up_at + up_part],
            dy_ref[:, k * up_part : (k + 1) * up_part],
            NT,
        )
    scaled = adapter_scale * back_t
    back = scaled.astype(jnp.bfloat16)
    back_ref[...] = scaled.T.astype(jnp.bfloat16)
    for k in range(shares):
        x = x_ref[:, k * down_part : (k + 1) * down_part]
        low_t += dot(fac_ref[k, :, :down_part], x, NT)
        grads_ref[k, :, :down_part] = dot(back, x).astype(jnp.bfloat16)
        grads_ref[k, :, back_at:] = back
    low = low_t.astype(jnp.bfloat16)
    for k in range(shares):
        grads_ref[k, :, up_at : up_at + up_part] = (
            adapter_scale * dot(low, dy_ref[:, k * up_part : (k + 1) * up_part])
        ).astype(jnp.bfloat16)


def owner_kernel(slots, me_ref, apb_ref, row_ref, got_ref, out_ref, acc_ref):
    blocks = got_ref.shape[0]
    acc_ref[...] = jnp.zeros_like(acc_ref)
    for j in range(blocks):
        owner = lax.div(row_ref[apb_ref[me_ref[0] * blocks + j]], slots)
        acc_ref[owner] += got_ref[j, :, : acc_ref.shape[2]].astype(jnp.float32)
    out_ref[...] = acc_ref[...].astype(jnp.bfloat16)


def total_kernel(want_ref, count_ref, got_ref, down_ref, up_ref):
    slots, _, down_part = down_ref.shape
    up_part = up_ref.shape[2]
    up_at = round_up(down_part)
    down_ref[...] = jnp.zeros_like(down_ref)
    up_ref[...] = jnp.zeros_like(up_ref)

    def group(g, carry):
        slot = want_ref[g]
        down_ref[slot] += got_ref[g, :, :down_part].astype(jnp.float32)
        up_ref[slot] += got_ref[g, :, up_at : up_at + up_part].astype(jnp.float32)
        return carry

    lax.fori_loop(0, got_ref.shape[0], group, 0)
    for s in range(slots):
        divisor = jnp.maximum(count_ref[s], 1).astype(jnp.float32)
        down_ref[s] = down_ref[s] / divisor
        up_ref[s] = up_ref[s] / divisor


def far_kernel(
    near, at_ref, w_hbm, y2_hbm, y3_hbm, share_ref, got_ref, z2_ref, z3_ref, w_ref, dy_ref, sems
):
    rows = z2_ref.shape[1]
    tokens = z2_ref.shape[0]
    taken = pl.ds(y2_hbm.shape[0] - tokens, tokens)
    copies = fetch(
        [y2_hbm.at[taken], y3_hbm.at[taken], w_hbm.at[pl.ds(near, rows)]],
        [dy_ref.at[pl.ds(0, tokens)], dy_ref.at[pl.ds(tokens, tokens)], w_ref],
        sems,
    )
    copies[0].wait()
    copies[1].wait()
    dy_t = turned(dy_ref[...])
    copies[2].wait()
    frozen_t = dot(w_ref[...], dy_t)
    for i, z_ref in enumerate((z2_ref, z3_ref)):
        peer = lax.bitwise_xor(at_ref[0], 2 + i)
        back = turned(got_ref[peer, :, got_ref.shape[2] - tokens :])
        z_ref[...] = (
            frozen_t[:, i * tokens : (i + 1) * tokens].T
            + dot(back, share_ref[peer, :, near : near + rows])
        ).astype(jnp.bfloat16)


def input_kernel(
    at_ref, side_ref, back_ref, fac_ref, dy_hbm, y2_hbm, y3_hbm, x2_hbm, x3_hbm, w0_hbm, w1_hbm,
    out_ref, dy_ref, few_ref, w0_ref, w1_ref, buf, fetch_sems, sems,
):
    part = w0_ref.shape[0]
    taken = few_ref.shape[1]
    side = side_ref[0] * taken
    few = [a.at[pl.ds(0, taken)] for a in (y2_hbm, y3_hbm, x2_hbm, x3_hbm)]
    fetches = fetch(
        (*few, w0_hbm, w1_hbm, dy_hbm),
        (*(few_ref.at[i] for i in range(4)), w0_ref, w1_ref, dy_ref),
        fetch_sems,
    )
    fetches[6].wait()
    dy_t = turned(dy_ref[...])
    copies = []
    for i, (k, w_ref, start, rows) in enumerate(
        (
            (2, few_ref.at[0], side, taken),
            (3, few_ref.at[1], side, taken),
            (2, few_ref.at[2], taken - side, taken),
            (3, few_ref.at[3], taken - side, taken),
            (0, w0_ref, 0, part),
            (1, w1_ref, 0, part),
        )
    ):
        fetches[i].wait()
        peer = lax.bitwise_xor(at_ref[0], k)
        start = pl.multiple_of(start, LANES)
        buf[i, :, :rows] = (
            dot(w_ref[...], dy_t).T
            + dot(back_ref[...], fac_ref[peer, :, pl.ds(start, rows)])
        ).astype(jnp.bfloat16)
        first = pl.multiple_of(peer * part + start, LANES)
        copy = pltpu.make_async_copy(
            buf.at[i, :, pl.ds(0, rows)], out_ref.at[:, pl.ds(first, rows)], sems.at[i]
        )
        copy.start()
        copies.append(copy)
    for copy in copies:
        copy.wait()


def place_kernel(at_ref, z2_ref, z3_ref, in_ref, out_ref, sems):
    rows = z2_ref.shape[1]
    part = out_ref.shape[1] // 4
    copies = []
    for i, z_ref in enumerate((z2_ref, z3_ref)):
        peer = lax.bitwise_xor(at_ref[0], 2 + i)
        first = pl.multiple_of(peer * part + (part - rows), LANES)
        copy = pltpu.make_async_copy(z_ref, out_ref.at[:, pl.ds(first, rows)], sems.at[i])
        copy.start()
        copies.append(copy)
    for copy in copies:
        copy.wait()


def in_hbm(*arrays):
    return [pltpu.with_memory_space_constraint(a, pltpu.HBM) for a in arrays]


def call(
    kernel, out_shape, out_specs, *operands, smem=0, scratch=(), vmem=8, specs=None, aliases=None
):
    return pl.pallas_call(
        kernel,
        out_shape=out_shape,
        in_specs=[SMEM] * smem + (specs or [VMEM] * (len(operands) - smem)),
        input_output_aliases=aliases or {},
        out_specs=out_specs,
        scratch_shapes=scratch,
        compiler_params=pltpu.CompilerParams(vmem_limit_bytes=vmem << 20),
    )(*operands)


def per_device(
    projection_input,
    value_cotangent,
    value_weight,
    adapter_down_table,
    adapter_up_table,
    adapter_per_block,
    adapter_table_row,
):
    dp_count = lax.axis_size("dp")
    fsdp_count = lax.axis_size("fsdp")
    me = lax.axis_index("dp").reshape(1)
    at = lax.axis_index("fsdp")
    tok_rows, width = projection_input.shape
    slots, rank, down_part = adapter_down_table.shape
    up_part = adapter_up_table.shape[2]
    assert tok_rows == BLOCK
    wide = round_up(down_part) + round_up(up_part)
    bf16 = jnp.bfloat16

    def shaped(*shape, dtype=bf16):
        return jax.ShapeDtypeStruct(shape, dtype)

    by_permute = fsdp_count == 4 and down_part % 256 == 0
    by_permute = by_permute and dp_count % 2 == 0
    side_rows = down_part // 4 // LANES * LANES
    near_rows = 2 * side_rows

    def cross(array, bit, axis="fsdp"):
        return lax.ppermute(array, axis, [(i, i ^ bit) for i in range(lax.axis_size(axis))])

    index = (me, adapter_per_block, adapter_table_row)
    send, want, count = call(
        functools.partial(pick_kernel, fsdp_count),
        (
            shaped(dp_count, rank, wide),
            shaped(dp_count, dtype=jnp.int32),
            shaped(slots, dtype=jnp.int32),
        ),
        (VMEM, SMEM, SMEM),
        me,
        *in_hbm(*index[1:], adapter_down_table, adapter_up_table),
        smem=1,
        specs=[ANY] * 4,
        scratch=[
            pltpu.SMEM(adapter_per_block.shape, jnp.int32),
            pltpu.SMEM(adapter_table_row.shape, jnp.int32),
            pltpu.VMEM(adapter_down_table.shape, bf16),
            pltpu.VMEM(adapter_up_table.shape, bf16),
            pltpu.SemaphoreType.DMA((4,)),
        ],
    )
    if by_permute:
        value_weight, send = lax.optimization_barrier((value_weight, send))
    owned = lax.all_to_all(send, "dp", split_axis=0, concat_axis=0, tiled=True)
    if by_permute:
        side = me & 1
        some = lax.dynamic_slice_in_dim(value_weight, side[0] * side_rows, side_rows, 0)
        y2 = cross(jnp.concatenate([some, value_cotangent], axis=0), 2)
        at_hand, _ = lax.optimization_barrier((projection_input, send))
        at_hand = call(
            copy_kernel,
            shaped(tok_rows, width),
            ANY,
            *in_hbm(at_hand),
            specs=[ANY],
            scratch=[pltpu.SemaphoreType.DMA],
        )
        owned, y2, at_hand = lax.optimization_barrier((owned, y2, at_hand))
        near = cross(value_weight, 1), cross(y2, 1)
    else:
        at_hand = projection_input
    share = call(
        functools.partial(share_kernel, slots),
        shaped(fsdp_count, rank, wide),
        VMEM,
        *index,
        owned,
        smem=3,
    )
    if by_permute:
        x2, share = lax.optimization_barrier((y2, share))
        x2 = cross(x2, 1, "dp")
    factors = lax.all_to_all(share, "fsdp", split_axis=0, concat_axis=0, tiled=True)
    grads, back = call(
        functools.partial(block_kernel, down_part, up_part),
        (
            shaped(fsdp_count, rank, wide + BLOCK),
            shaped(BLOCK, rank),
        ),
        (VMEM, VMEM),
        at_hand,
        value_cotangent,
        factors,
        vmem=20,
    )
    got = lax.all_to_all(grads, "fsdp", split_axis=0, concat_axis=0, tiled=True)
    if by_permute:
        got, x2, near = lax.optimization_barrier((got, x2, near))
        x3 = cross(x2, 1)
    sums = call(
        functools.partial(owner_kernel, slots),
        shaped(dp_count, rank, wide),
        VMEM,
        *index,
        got,
        smem=3,
        scratch=[pltpu.VMEM((dp_count, rank, wide), jnp.float32)],
    )
    arrived = lax.all_to_all(sums, "dp", split_axis=0, concat_axis=0, tiled=True)
    if by_permute:
        at = at.reshape(1)
        far_rows = down_part - near_rows
        z2, z3 = call(
            functools.partial(far_kernel, near_rows),
            (shaped(BLOCK, far_rows), shaped(BLOCK, far_rows)),
            (VMEM, VMEM),
            at,
            *in_hbm(value_weight, y2, near[1]),
            share,
            got,
            smem=1,
            specs=[ANY] * 3 + [VMEM] * 2,
            vmem=20,
            scratch=[
                pltpu.VMEM((far_rows, value_weight.shape[1]), bf16),
                pltpu.VMEM((2 * BLOCK, value_weight.shape[1]), bf16),
                pltpu.SemaphoreType.DMA((3,)),
            ],
        )
        z2, z3 = cross(z2, 2), cross(z3, 3)
        grad_input = call(
            input_kernel,
            shaped(tok_rows, width),
            pl.BlockSpec(memory_space=pl.ANY),
            at,
            side,
            back,
            factors,
            *in_hbm(value_cotangent, y2, near[1], x2, x3, value_weight, near[0]),
            smem=2,
            specs=[VMEM] * 2 + [ANY] * 7,
            vmem=24,
            scratch=[
                pltpu.VMEM(value_cotangent.shape, bf16),
                pltpu.VMEM((4, side_rows, value_weight.shape[1]), bf16),
                pltpu.VMEM(value_weight.shape, bf16),
                pltpu.VMEM(value_weight.shape, bf16),
                pltpu.VMEM((6, tok_rows, down_part), bf16),
                pltpu.SemaphoreType.DMA((7,)),
                pltpu.SemaphoreType.DMA((6,)),
            ],
        )
        grad_input = call(
            place_kernel,
            shaped(tok_rows, width),
            pl.BlockSpec(memory_space=pl.ANY),
            at,
            z2,
            z3,
            grad_input,
            smem=1,
            specs=[VMEM, VMEM, pl.BlockSpec(memory_space=pl.ANY)],
            scratch=[pltpu.SemaphoreType.DMA((2,))],
            aliases={3: 0},
        )
        arrived, grad_input = lax.optimization_barrier((arrived, grad_input))
    grad_down, grad_up = call(
        total_kernel,
        (
            shaped(slots, rank, down_part, dtype=jnp.float32),
            shaped(slots, rank, up_part, dtype=jnp.float32),
        ),
        (VMEM, VMEM),
        want,
        count,
        arrived,
        smem=2,
    )
    if not by_permute:
        weight = lax.all_gather(value_weight, "fsdp", axis=0, tiled=True)
        adapter_term = jnp.einsum(
            "tr,krd->tkd", back, factors[:, :, :down_part], preferred_element_type=jnp.float32
        )
        frozen_term = jnp.einsum(
            "tc,dc->td", value_cotangent, weight, preferred_element_type=jnp.float32
        )
        grad_input = (frozen_term + adapter_term.reshape(tok_rows, width)).astype(bf16)
    return (grad_input, grad_down, grad_up)


def solution(mesh):
    return jax.shard_map(
        per_device,
        mesh=mesh,
        in_specs=(
            P(("dp", "fsdp"), None),
            P(("dp", "fsdp"), None),
            P("fsdp", None),
            P("dp", None, "fsdp"),
            P("dp", None, "fsdp"),
            P(),
            P(),
        ),
        out_specs=(P(("dp", "fsdp"), None), P("dp", None, "fsdp"), P("dp", None, "fsdp")),
        check_vma=False,
    )
```

```python
import functools

import jax
import jax.numpy as jnp
from jax import lax
from jax.experimental import pallas as pl
from jax.experimental.pallas import tpu as pltpu
from jax.sharding import PartitionSpec as P

BLOCK = 128
LANES = 128
adapter_scale = 2.0

SMEM = pl.BlockSpec(memory_space=pltpu.SMEM)
VMEM = pl.BlockSpec(memory_space=pltpu.VMEM)
ANY = pl.BlockSpec(memory_space=pl.ANY)
NT = (((1,), (1,)), ((), ()))


def round_up(n):
    return -(-n // LANES) * LANES


def dot(a, b, dims=(((1,), (0,)), ((), ()))):
    return lax.dot_general(a, b, dims, preferred_element_type=jnp.float32)


def turned(a):
    return a.astype(jnp.float32).T.astype(a.dtype)


def fetch(sources, targets, sems):
    copies = [
        pltpu.make_async_copy(source, target, sems.at[i])
        for i, (source, target) in enumerate(zip(sources, targets))
    ]
    for copy in copies:
        copy.start()
    return copies


def copy_kernel(from_ref, to_ref, sem):
    copy = pltpu.make_async_copy(from_ref, to_ref, sem)
    copy.start()
    copy.wait()


def pick_kernel(
    group_blocks, me_ref, apb_hbm, row_hbm, down_hbm, up_hbm, w_hbm, send_ref, want_ref,
    count_ref, some_ref, apb_ref, row_ref, down_ref, up_ref, sems,
):
    rows = some_ref.shape[0]
    start = pl.multiple_of(lax.rem(me_ref[0], 2) * rows, 16)
    copies = fetch(
        (apb_hbm, row_hbm, down_hbm, up_hbm, w_hbm.at[pl.ds(start, rows)]),
        (
            apb_ref,
            row_ref,
            down_ref,
            up_ref,
            some_ref,
        ),
        sems,
    )
    slots, _, down_part = down_ref.shape
    up_part = up_ref.shape[2]
    up_at = round_up(down_part)
    groups = send_ref.shape[0]
    first = me_ref[0] * slots
    for s in range(slots):
        count_ref[s] = 0
    copies[0].wait()
    copies[1].wait()

    def group(g, carry):
        want_ref[g] = 0
        for j in range(group_blocks):
            local = row_ref[apb_ref[g * group_blocks + j]] - first

            @pl.when((local >= 0) & (local < slots))
            def _():
                want_ref[g] = local
                count_ref[local] = count_ref[local] + 1

        return carry

    lax.fori_loop(0, groups, group, 0)
    copies[2].wait()
    copies[3].wait()

    def put(g, carry):
        slot = want_ref[g]
        send_ref[g, :, :down_part] = down_ref[slot]
        send_ref[g, :, up_at : up_at + up_part] = up_ref[slot]
        return carry

    lax.fori_loop(0, groups, put, 0)
    copies[4].wait()


def share_kernel(slots, me_ref, apb_ref, row_ref, got_ref, out_ref):
    blocks = out_ref.shape[0]
    for j in range(blocks):
        owner = lax.div(row_ref[apb_ref[me_ref[0] * blocks + j]], slots)
        out_ref[j] = got_ref[owner]


def block_kernel(
    down_part, up_part, x_ref, dy_ref, fac_ref, grads_ref, back_ref
):
    shares = fac_ref.shape[0]
    up_at = round_up(down_part)
    back_at = up_at + round_up(up_part)
    low_t = jnp.zeros((fac_ref.shape[1], BLOCK), jnp.float32)
    back_t = jnp.zeros((fac_ref.shape[1], BLOCK), jnp.float32)
    for k in range(shares):
        back_t += dot(
            fac_ref[k, :, up_at : up_at + up_part],
            dy_ref[:, k * up_part : (k + 1) * up_part],
            NT,
        )
    scaled = adapter_scale * back_t
    back = scaled.astype(jnp.bfloat16)
    back_ref[...] = scaled.T.astype(jnp.bfloat16)
    for k in range(shares):
        x = x_ref[:, k * down_part : (k + 1) * down_part]
        low_t += dot(fac_ref[k, :, :down_part], x, NT)
        grads_ref[k, :, :down_part] = dot(back, x).astype(jnp.bfloat16)
        grads_ref[k, :, back_at:] = back
    low = low_t.astype(jnp.bfloat16)
    for k in range(shares):
        grads_ref[k, :, up_at : up_at + up_part] = (
            adapter_scale * dot(low, dy_ref[:, k * up_part : (k + 1) * up_part])
        ).astype(jnp.bfloat16)


def owner_kernel(slots, me_ref, apb_ref, row_ref, got_ref, out_ref, total_ref):
    blocks = got_ref.shape[0]
    wide = out_ref.shape[2]
    owners = [
        lax.div(row_ref[apb_ref[me_ref[0] * blocks + j]], slots) for j in range(blocks)
    ]
    out_ref[...] = jnp.zeros_like(out_ref)
    for j in range(blocks):
        total_ref[...] = got_ref[j, :, :wide].astype(jnp.float32)
        for i in range(blocks):
            if i != j:

                @pl.when(owners[i] == owners[j])
                def _():
                    total_ref[...] += got_ref[i, :, :wide].astype(jnp.float32)

        out_ref[owners[j]] = total_ref[...].astype(jnp.bfloat16)


def total_kernel(want_ref, count_ref, got_ref, down_ref, up_ref):
    slots, _, down_part = down_ref.shape
    up_part = up_ref.shape[2]
    up_at = round_up(down_part)
    down_ref[...] = jnp.zeros_like(down_ref)
    up_ref[...] = jnp.zeros_like(up_ref)

    def group(g, carry):
        slot = want_ref[g]
        down_ref[slot] += got_ref[g, :, :down_part].astype(jnp.float32)
        up_ref[slot] += got_ref[g, :, up_at : up_at + up_part].astype(jnp.float32)
        return carry

    lax.fori_loop(0, got_ref.shape[0], group, 0)
    for s in range(slots):
        divisor = jnp.maximum(count_ref[s], 1).astype(jnp.float32)
        down_ref[s] = down_ref[s] / divisor
        up_ref[s] = up_ref[s] / divisor


def far_kernel(near, bits, at_ref, w_hbm, dy_ref, share_ref, got_ref, z_ref, w_ref, sems):
    tokens, rows = z_ref.shape
    copies = fetch([w_hbm.at[pl.ds(near, rows)]], [w_ref], sems)
    peer = lax.bitwise_xor(at_ref[0], bits)
    dy_t = turned(dy_ref[...])
    back = turned(got_ref[peer, :, got_ref.shape[2] - tokens :])
    adapted = dot(back, share_ref[peer, :, near : near + rows])
    copies[0].wait()
    z_ref[...] = (dot(w_ref[...], dy_t).T + adapted).astype(jnp.bfloat16)


def input_kernel(
    at_ref, side_ref, back_ref, fac_ref, dy_hbm, y2_hbm, y3_hbm, x2_hbm, x3_hbm, w0_hbm, w1_hbm,
    out_ref, dy_ref, few_ref, w0_ref, w1_ref, buf, fetch_sems, sems,
):
    part = w0_ref.shape[0]
    taken = few_ref.shape[1]
    side = side_ref[0] * taken
    few = [a.at[pl.ds(0, taken)] for a in (y2_hbm, y3_hbm, x2_hbm, x3_hbm)]
    fetches = fetch(
        (*few, w0_hbm, w1_hbm, dy_hbm),
        (*(few_ref.at[i] for i in range(4)), w0_ref, w1_ref, dy_ref),
        fetch_sems,
    )
    fetches[6].wait()
    dy_t = turned(dy_ref[...])
    copies = []
    for i, (k, w_ref, start, rows) in enumerate(
        (
            (2, few_ref.at[0], side, taken),
            (3, few_ref.at[1], side, taken),
            (2, few_ref.at[2], taken - side, taken),
            (3, few_ref.at[3], taken - side, taken),
            (0, w0_ref, 0, part),
            (1, w1_ref, 0, part),
        )
    ):
        fetches[i].wait()
        peer = lax.bitwise_xor(at_ref[0], k)
        start = pl.multiple_of(start, LANES)
        buf[i, :, :rows] = (
            dot(w_ref[...], dy_t).T
            + dot(back_ref[...], fac_ref[peer, :, pl.ds(start, rows)])
        ).astype(jnp.bfloat16)
        first = pl.multiple_of(peer * part + start, LANES)
        copy = pltpu.make_async_copy(
            buf.at[i, :, pl.ds(0, rows)], out_ref.at[:, pl.ds(first, rows)], sems.at[i]
        )
        copy.start()
        copies.append(copy)
    for copy in copies:
        copy.wait()


def place_kernel(at_ref, z2_ref, z3_ref, in_ref, out_ref, sems):
    rows = z2_ref.shape[1]
    part = out_ref.shape[1] // 4
    copies = []
    for i, z_ref in enumerate((z2_ref, z3_ref)):
        peer = lax.bitwise_xor(at_ref[0], 2 + i)
        first = pl.multiple_of(peer * part + (part - rows), LANES)
        copy = pltpu.make_async_copy(z_ref, out_ref.at[:, pl.ds(first, rows)], sems.at[i])
        copy.start()
        copies.append(copy)
    for copy in copies:
        copy.wait()


def in_hbm(*arrays):
    return [pltpu.with_memory_space_constraint(a, pltpu.HBM) for a in arrays]


def call(
    kernel, out_shape, out_specs, *operands, smem=0, scratch=(), vmem=8, specs=None, aliases=None
):
    return pl.pallas_call(
        kernel,
        out_shape=out_shape,
        in_specs=[SMEM] * smem + (specs or [VMEM] * (len(operands) - smem)),
        input_output_aliases=aliases or {},
        out_specs=out_specs,
        scratch_shapes=scratch,
        compiler_params=pltpu.CompilerParams(vmem_limit_bytes=vmem << 20),
    )(*operands)


def per_device(
    projection_input,
    value_cotangent,
    value_weight,
    adapter_down_table,
    adapter_up_table,
    adapter_per_block,
    adapter_table_row,
):
    dp_count = lax.axis_size("dp")
    fsdp_count = lax.axis_size("fsdp")
    me = lax.axis_index("dp").reshape(1)
    at = lax.axis_index("fsdp")
    tok_rows, width = projection_input.shape
    slots, rank, down_part = adapter_down_table.shape
    up_part = adapter_up_table.shape[2]
    assert tok_rows == BLOCK
    wide = round_up(down_part) + round_up(up_part)
    bf16 = jnp.bfloat16

    def shaped(*shape, dtype=bf16):
        return jax.ShapeDtypeStruct(shape, dtype)

    by_permute = fsdp_count == 4 and down_part % 256 == 0
    by_permute = by_permute and dp_count % 2 == 0
    side_rows = round_up(down_part // 4) if by_permute else 16
    near_rows = 2 * side_rows

    def cross(array, bit, axis="fsdp"):
        return lax.ppermute(array, axis, [(i, i ^ bit) for i in range(lax.axis_size(axis))])

    index = (me, adapter_per_block, adapter_table_row)
    send, want, count, some = call(
        functools.partial(pick_kernel, fsdp_count),
        (
            shaped(dp_count, rank, wide),
            shaped(dp_count, dtype=jnp.int32),
            shaped(slots, dtype=jnp.int32),
            shaped(side_rows, value_weight.shape[1]),
        ),
        (VMEM, SMEM, SMEM, VMEM),
        me,
        *in_hbm(*index[1:], adapter_down_table, adapter_up_table, value_weight),
        smem=1,
        specs=[ANY] * 5,
        scratch=[
            pltpu.SMEM(adapter_per_block.shape, jnp.int32),
            pltpu.SMEM(adapter_table_row.shape, jnp.int32),
            pltpu.VMEM(adapter_down_table.shape, bf16),
            pltpu.VMEM(adapter_up_table.shape, bf16),
            pltpu.SemaphoreType.DMA((5,)),
        ],
    )
    owned = lax.all_to_all(send, "dp", split_axis=0, concat_axis=0, tiled=True)
    if by_permute:
        side = me & 1
        y2 = cross(some, 2)
        dy2 = cross(value_cotangent, 2)
        at_hand, _ = lax.optimization_barrier((projection_input, send))
        at_hand = call(
            copy_kernel,
            shaped(tok_rows, width),
            VMEM,
            *in_hbm(at_hand),
            specs=[ANY],
            scratch=[pltpu.SemaphoreType.DMA],
        )
        owned, y2, at_hand = lax.optimization_barrier((owned, y2, at_hand))
    else:
        at_hand = projection_input
    share = call(
        functools.partial(share_kernel, slots),
        shaped(fsdp_count, rank, wide),
        VMEM,
        *index,
        owned,
        smem=3,
    )
    if by_permute:
        x2, share, dy2, beside = lax.optimization_barrier((y2, share, dy2, value_weight))
        near = cross(beside, 1), cross(x2, 1)
        x2 = cross(x2, 1, "dp")
    factors = lax.all_to_all(share, "fsdp", split_axis=0, concat_axis=0, tiled=True)
    grads, back = call(
        functools.partial(block_kernel, down_part, up_part),
        (
            shaped(fsdp_count, rank, wide + BLOCK),
            shaped(BLOCK, rank),
        ),
        (VMEM, VMEM),
        at_hand,
        value_cotangent,
        factors,
        vmem=20,
    )
    got = lax.all_to_all(grads, "fsdp", split_axis=0, concat_axis=0, tiled=True)
    if by_permute:
        got, x2, near = lax.optimization_barrier((got, x2, near))
        got, dy2 = lax.optimization_barrier((got, dy2))
        x3, dy3 = cross(x2, 1), cross(dy2, 1)
    sums = call(
        functools.partial(owner_kernel, slots),
        shaped(dp_count, rank, wide),
        VMEM,
        *index,
        got,
        smem=3,
        scratch=[pltpu.VMEM((rank, wide), jnp.float32)],
    )
    arrived = lax.all_to_all(sums, "dp", split_axis=0, concat_axis=0, tiled=True)
    if by_permute:
        at = at.reshape(1)
        far_rows = down_part - near_rows
        z2, z3 = (
            cross(
                call(
                    functools.partial(far_kernel, near_rows, bits),
                    shaped(BLOCK, far_rows),
                    VMEM,
                    at,
                    *in_hbm(value_weight),
                    dy,
                    share,
                    got,
                    smem=1,
                    specs=[ANY] + [VMEM] * 3,
                    vmem=12,
                    scratch=[
                        pltpu.VMEM((far_rows, value_weight.shape[1]), bf16),
                        pltpu.SemaphoreType.DMA((1,)),
                    ],
                ),
                bits,
            )
            for bits, dy in ((2, dy2), (3, dy3))
        )
        grad_input = call(
            input_kernel,
            shaped(tok_rows, width),
            pl.BlockSpec(memory_space=pl.ANY),
            at,
            side,
            back,
            factors,
            *in_hbm(value_cotangent, y2),
            near[1],
            *in_hbm(x2),
            x3,
            *in_hbm(value_weight, near[0]),
            smem=2,
            specs=[VMEM] * 2 + [ANY] * 7,
            vmem=24,
            scratch=[
                pltpu.VMEM(value_cotangent.shape, bf16),
                pltpu.VMEM((4, side_rows, value_weight.shape[1]), bf16),
                pltpu.VMEM(value_weight.shape, bf16),
                pltpu.VMEM(value_weight.shape, bf16),
                pltpu.VMEM((6, tok_rows, down_part), bf16),
                pltpu.SemaphoreType.DMA((7,)),
                pltpu.SemaphoreType.DMA((6,)),
            ],
        )
        grad_input = call(
            place_kernel,
            shaped(tok_rows, width),
            pl.BlockSpec(memory_space=pl.ANY),
            at,
            z2,
            z3,
            grad_input,
            smem=1,
            specs=[VMEM, VMEM, pl.BlockSpec(memory_space=pl.ANY)],
            scratch=[pltpu.SemaphoreType.DMA((2,))],
            aliases={3: 0},
        )
        arrived, grad_input = lax.optimization_barrier((arrived, grad_input))
    grad_down, grad_up = call(
        total_kernel,
        (
            shaped(slots, rank, down_part, dtype=jnp.float32),
            shaped(slots, rank, up_part, dtype=jnp.float32),
        ),
        (VMEM, VMEM),
        want,
        count,
        arrived,
        smem=2,
    )
    if not by_permute:
        weight = lax.all_gather(value_weight, "fsdp", axis=0, tiled=True)
        adapter_term = jnp.einsum(
            "tr,krd->tkd", back, factors[:, :, :down_part], preferred_element_type=jnp.float32
        )
        frozen_term = jnp.einsum(
            "tc,dc->td", value_cotangent, weight, preferred_element_type=jnp.float32
        )
        grad_input = (frozen_term + adapter_term.reshape(tok_rows, width)).astype(bf16)
    return (grad_input, grad_down, grad_up)


def solution(mesh):
    return jax.shard_map(
        per_device,
        mesh=mesh,
        in_specs=(
            P(("dp", "fsdp"), None),
            P(("dp", "fsdp"), None),
            P("fsdp", None),
            P("dp", None, "fsdp"),
            P("dp", None, "fsdp"),
            P(),
            P(),
        ),
        out_specs=(P(("dp", "fsdp"), None), P("dp", None, "fsdp"), P("dp", None, "fsdp")),
        check_vma=False,
    )
```

```python
import functools

import jax
import jax.numpy as jnp
from jax import lax
from jax.experimental import pallas as pl
from jax.experimental.pallas import tpu as pltpu
from jax.sharding import PartitionSpec as P

BLOCK = 128
LANES = 128
adapter_scale = 2.0

SMEM = pl.BlockSpec(memory_space=pltpu.SMEM)
VMEM = pl.BlockSpec(memory_space=pltpu.VMEM)
ANY = pl.BlockSpec(memory_space=pl.ANY)
NT = (((1,), (1,)), ((), ()))


def round_up(n):
    return -(-n // LANES) * LANES


def dot(a, b, dims=(((1,), (0,)), ((), ()))):
    return lax.dot_general(a, b, dims, preferred_element_type=jnp.float32)


def turned(a):
    return a.astype(jnp.float32).T.astype(a.dtype)


def fetch(sources, targets, sems):
    copies = [
        pltpu.make_async_copy(source, target, sems.at[i])
        for i, (source, target) in enumerate(zip(sources, targets))
    ]
    for copy in copies:
        copy.start()
    return copies


def copy_kernel(from_ref, to_ref, sem):
    copy = pltpu.make_async_copy(from_ref, to_ref, sem)
    copy.start()
    copy.wait()


def pick_kernel(
    group_blocks, me_ref, apb_hbm, row_hbm, down_hbm, up_hbm, w_hbm, send_ref, want_ref,
    count_ref, some_ref, apb_ref, row_ref, down_ref, up_ref, sems,
):
    rows = some_ref.shape[0]
    start = pl.multiple_of(lax.rem(me_ref[0], 2) * rows, 16)
    copies = fetch(
        (apb_hbm, row_hbm, down_hbm, up_hbm, w_hbm.at[pl.ds(start, rows)]),
        (
            apb_ref,
            row_ref,
            down_ref,
            up_ref,
            some_ref,
        ),
        sems,
    )
    slots, _, down_part = down_ref.shape
    up_part = up_ref.shape[2]
    up_at = round_up(down_part)
    groups = send_ref.shape[0]
    first = me_ref[0] * slots
    for s in range(slots):
        count_ref[s] = 0
    copies[0].wait()
    copies[1].wait()

    def group(g, carry):
        want_ref[g] = 0
        for j in range(group_blocks):
            local = row_ref[apb_ref[g * group_blocks + j]] - first

            @pl.when((local >= 0) & (local < slots))
            def _():
                want_ref[g] = local
                count_ref[local] = count_ref[local] + 1

        return carry

    lax.fori_loop(0, groups, group, 0)
    copies[2].wait()
    copies[3].wait()

    def put(g, carry):
        slot = want_ref[g]
        send_ref[g, :, :down_part] = down_ref[slot]
        send_ref[g, :, up_at : up_at + up_part] = up_ref[slot]
        return carry

    lax.fori_loop(0, groups, put, 0)
    copies[4].wait()


def peer_of(by_xor, at_ref, k):
    return lax.bitwise_xor(at_ref[0], k) if by_xor else k


def columns(ref, peer, width):
    if isinstance(peer, int):
        return ref[:, peer * width : (peer + 1) * width]
    return ref[:, pl.ds(pl.multiple_of(peer * width, LANES), width)]


def share_kernel(by_xor, slots, at_ref, me_ref, apb_ref, row_ref, got_ref, *out_refs):
    blocks = len(out_refs)
    for k, out_ref in enumerate(out_refs):
        block = me_ref[0] * blocks + peer_of(by_xor, at_ref, k)
        out_ref[...] = got_ref[lax.div(row_ref[apb_ref[block]], slots)]


def block_kernel(by_xor, down_part, up_part, shares, at_ref, x_ref, dy_ref, *refs):
    fac_refs, grads_refs, back_ref = refs[:shares], refs[shares:-1], refs[-1]
    up_at = round_up(down_part)
    wide = up_at + round_up(up_part)
    peers = [peer_of(by_xor, at_ref, k) for k in range(shares)]
    rank = fac_refs[0].shape[0]
    low_t = jnp.zeros((rank, BLOCK), jnp.float32)
    back_t = jnp.zeros((rank, BLOCK), jnp.float32)
    for k in range(shares):
        back_t += dot(
            fac_refs[k][:, up_at : up_at + up_part], columns(dy_ref, peers[k], up_part), NT
        )
    scaled = adapter_scale * back_t
    back = scaled.astype(jnp.bfloat16)
    back_ref[...] = scaled.T.astype(jnp.bfloat16)
    for k in range(shares):
        x = columns(x_ref, peers[k], down_part)
        low_t += dot(fac_refs[k][:, :down_part], x, NT)
        grads_refs[k][:, :down_part] = dot(back, x).astype(jnp.bfloat16)
        grads_refs[k][:, wide:] = back
    low = low_t.astype(jnp.bfloat16)
    for k in range(shares):
        grads_refs[k][:, up_at : up_at + up_part] = (
            adapter_scale * dot(low, columns(dy_ref, peers[k], up_part))
        ).astype(jnp.bfloat16)


def owner_kernel(by_xor, slots, at_ref, me_ref, apb_ref, row_ref, *refs):
    got_refs, out_ref, total_ref = refs[:-2], refs[-2], refs[-1]
    blocks = len(got_refs)
    wide = out_ref.shape[2]
    owners = [
        lax.div(row_ref[apb_ref[me_ref[0] * blocks + peer_of(by_xor, at_ref, k)]], slots)
        for k in range(blocks)
    ]
    out_ref[...] = jnp.zeros_like(out_ref)
    for j in range(blocks):
        total_ref[...] = got_refs[j][:, :wide].astype(jnp.float32)
        for i in range(blocks):
            if i != j:

                @pl.when(owners[i] == owners[j])
                def _():
                    total_ref[...] += got_refs[i][:, :wide].astype(jnp.float32)

        out_ref[owners[j]] = total_ref[...].astype(jnp.bfloat16)


def total_kernel(want_ref, count_ref, got_ref, down_ref, up_ref):
    slots, _, down_part = down_ref.shape
    up_part = up_ref.shape[2]
    up_at = round_up(down_part)
    down_ref[...] = jnp.zeros_like(down_ref)
    up_ref[...] = jnp.zeros_like(up_ref)

    def group(g, carry):
        slot = want_ref[g]
        down_ref[slot] += got_ref[g, :, :down_part].astype(jnp.float32)
        up_ref[slot] += got_ref[g, :, up_at : up_at + up_part].astype(jnp.float32)
        return carry

    lax.fori_loop(0, got_ref.shape[0], group, 0)
    for s in range(slots):
        divisor = jnp.maximum(count_ref[s], 1).astype(jnp.float32)
        down_ref[s] = down_ref[s] / divisor
        up_ref[s] = up_ref[s] / divisor


def far_kernel(near, w_hbm, dy_ref, share_ref, got_ref, z_ref, w_ref, sems):
    tokens, rows = z_ref.shape
    copies = fetch([w_hbm.at[pl.ds(near, rows)]], [w_ref], sems)
    dy_t = turned(dy_ref[...])
    back = turned(got_ref[:, got_ref.shape[1] - tokens :])
    adapted = dot(back, share_ref[:, near : near + rows])
    copies[0].wait()
    z_ref[...] = (dot(w_ref[...], dy_t).T + adapted).astype(jnp.bfloat16)


def input_kernel(
    at_ref, side_ref, back_ref, fac0_ref, fac1_ref, fac2_ref, fac3_ref, dy_hbm, y2_hbm, y3_hbm, x2_hbm, x3_hbm, w0_hbm, w1_hbm,
    out_ref, dy_ref, few_ref, w0_ref, w1_ref, buf, fetch_sems, sems,
):
    part = w0_ref.shape[0]
    fac_refs = (fac0_ref, fac1_ref, fac2_ref, fac3_ref)
    taken = few_ref.shape[1]
    side = side_ref[0] * taken
    few = [a.at[pl.ds(0, taken)] for a in (y2_hbm, y3_hbm, x2_hbm, x3_hbm)]
    fetches = fetch(
        (*few, w0_hbm, w1_hbm, dy_hbm),
        (*(few_ref.at[i] for i in range(4)), w0_ref, w1_ref, dy_ref),
        fetch_sems,
    )
    fetches[6].wait()
    dy_t = turned(dy_ref[...])
    copies = []
    for i, (k, w_ref, start, rows) in enumerate(
        (
            (2, few_ref.at[0], side, taken),
            (3, few_ref.at[1], side, taken),
            (2, few_ref.at[2], taken - side, taken),
            (3, few_ref.at[3], taken - side, taken),
            (0, w0_ref, 0, part),
            (1, w1_ref, 0, part),
        )
    ):
        fetches[i].wait()
        peer = lax.bitwise_xor(at_ref[0], k)
        start = pl.multiple_of(start, LANES)
        buf[i, :, :rows] = (
            dot(w_ref[...], dy_t).T
            + dot(back_ref[...], fac_refs[k][:, pl.ds(start, rows)])
        ).astype(jnp.bfloat16)
        first = pl.multiple_of(peer * part + start, LANES)
        copy = pltpu.make_async_copy(
            buf.at[i, :, pl.ds(0, rows)], out_ref.at[:, pl.ds(first, rows)], sems.at[i]
        )
        copy.start()
        copies.append(copy)
    for copy in copies:
        copy.wait()


def place_kernel(at_ref, z2_ref, z3_ref, in_ref, out_ref, sems):
    rows = z2_ref.shape[1]
    part = out_ref.shape[1] // 4
    copies = []
    for i, z_ref in enumerate((z2_ref, z3_ref)):
        peer = lax.bitwise_xor(at_ref[0], 2 + i)
        first = pl.multiple_of(peer * part + (part - rows), LANES)
        copy = pltpu.make_async_copy(z_ref, out_ref.at[:, pl.ds(first, rows)], sems.at[i])
        copy.start()
        copies.append(copy)
    for copy in copies:
        copy.wait()


def in_hbm(*arrays):
    return [pltpu.with_memory_space_constraint(a, pltpu.HBM) for a in arrays]


def call(
    kernel, out_shape, out_specs, *operands, smem=0, scratch=(), vmem=8, specs=None, aliases=None
):
    return pl.pallas_call(
        kernel,
        out_shape=out_shape,
        in_specs=[SMEM] * smem + (specs or [VMEM] * (len(operands) - smem)),
        input_output_aliases=aliases or {},
        out_specs=out_specs,
        scratch_shapes=scratch,
        compiler_params=pltpu.CompilerParams(vmem_limit_bytes=vmem << 20),
    )(*operands)


def per_device(
    projection_input,
    value_cotangent,
    value_weight,
    adapter_down_table,
    adapter_up_table,
    adapter_per_block,
    adapter_table_row,
):
    dp_count = lax.axis_size("dp")
    fsdp_count = lax.axis_size("fsdp")
    me = lax.axis_index("dp").reshape(1)
    at = lax.axis_index("fsdp")
    tok_rows, width = projection_input.shape
    slots, rank, down_part = adapter_down_table.shape
    up_part = adapter_up_table.shape[2]
    assert tok_rows == BLOCK
    wide = round_up(down_part) + round_up(up_part)
    bf16 = jnp.bfloat16

    def shaped(*shape, dtype=bf16):
        return jax.ShapeDtypeStruct(shape, dtype)

    by_permute = fsdp_count == 4 and down_part % 256 == 0
    by_permute = by_permute and dp_count % 2 == 0
    side_rows = round_up(down_part // 4) if by_permute else 16
    near_rows = 2 * side_rows

    def cross(array, bit, axis="fsdp"):
        return lax.ppermute(array, axis, [(i, i ^ bit) for i in range(lax.axis_size(axis))])

    def exchange(arrays):
        if by_permute:
            return [cross(a, k) if k else a for k, a in enumerate(arrays)]
        stacked = lax.all_to_all(jnp.stack(arrays), "fsdp", split_axis=0, concat_axis=0, tiled=True)
        return [stacked[k] for k in range(fsdp_count)]

    at = at.reshape(1)
    index = (me, adapter_per_block, adapter_table_row)
    send, want, count, some = call(
        functools.partial(pick_kernel, fsdp_count),
        (
            shaped(dp_count, rank, wide),
            shaped(dp_count, dtype=jnp.int32),
            shaped(slots, dtype=jnp.int32),
            shaped(side_rows, value_weight.shape[1]),
        ),
        (VMEM, SMEM, SMEM, VMEM),
        me,
        *in_hbm(*index[1:], adapter_down_table, adapter_up_table, value_weight),
        smem=1,
        specs=[ANY] * 5,
        scratch=[
            pltpu.SMEM(adapter_per_block.shape, jnp.int32),
            pltpu.SMEM(adapter_table_row.shape, jnp.int32),
            pltpu.VMEM(adapter_down_table.shape, bf16),
            pltpu.VMEM(adapter_up_table.shape, bf16),
            pltpu.SemaphoreType.DMA((5,)),
        ],
    )
    owned = lax.all_to_all(send, "dp", split_axis=0, concat_axis=0, tiled=True)
    if by_permute:
        side = me & 1
        y2 = cross(some, 2)
        dy2 = cross(value_cotangent, 2)
        at_hand, _ = lax.optimization_barrier((projection_input, send))
        at_hand = call(
            copy_kernel,
            shaped(tok_rows, width),
            VMEM,
            *in_hbm(at_hand),
            specs=[ANY],
            scratch=[pltpu.SemaphoreType.DMA],
        )
        owned, y2, at_hand = lax.optimization_barrier((owned, y2, at_hand))
    else:
        at_hand = projection_input
    share = call(
        functools.partial(share_kernel, by_permute, slots),
        [shaped(rank, wide)] * fsdp_count,
        [VMEM] * fsdp_count,
        at,
        *index,
        owned,
        smem=4,
    )
    if by_permute:
        x2, share, dy2, beside = lax.optimization_barrier((y2, share, dy2, value_weight))
        near = cross(beside, 1), cross(x2, 1)
        x2 = cross(x2, 1, "dp")
    factors = exchange(share)
    *grads, back = call(
        functools.partial(block_kernel, by_permute, down_part, up_part, fsdp_count),
        [shaped(rank, wide + BLOCK)] * fsdp_count + [shaped(BLOCK, rank)],
        [VMEM] * (fsdp_count + 1),
        at,
        at_hand,
        value_cotangent,
        *factors,
        smem=1,
        vmem=20,
    )
    got = exchange(grads)
    if by_permute:
        got, x2, near = lax.optimization_barrier((got, x2, near))
        got, dy2 = lax.optimization_barrier((got, dy2))
        x3, dy3 = cross(x2, 1), cross(dy2, 1)
    sums = call(
        functools.partial(owner_kernel, by_permute, slots),
        shaped(dp_count, rank, wide),
        VMEM,
        at,
        *index,
        *got,
        smem=4,
        scratch=[pltpu.VMEM((rank, wide), jnp.float32)],
    )
    arrived = lax.all_to_all(sums, "dp", split_axis=0, concat_axis=0, tiled=True)
    if by_permute:
        far_rows = down_part - near_rows
        z2, z3 = (
            cross(
                call(
                    functools.partial(far_kernel, near_rows),
                    shaped(BLOCK, far_rows),
                    VMEM,
                    *in_hbm(value_weight),
                    dy,
                    share[bits],
                    got[bits],
                    specs=[ANY] + [VMEM] * 3,
                    vmem=12,
                    scratch=[
                        pltpu.VMEM((far_rows, value_weight.shape[1]), bf16),
                        pltpu.SemaphoreType.DMA((1,)),
                    ],
                ),
                bits,
            )
            for bits, dy in ((2, dy2), (3, dy3))
        )
        grad_input = call(
            input_kernel,
            shaped(tok_rows, width),
            pl.BlockSpec(memory_space=pl.ANY),
            at,
            side,
            back,
            *factors,
            *in_hbm(value_cotangent, y2),
            near[1],
            *in_hbm(x2),
            x3,
            *in_hbm(value_weight, near[0]),
            smem=2,
            specs=[VMEM] * 5 + [ANY] * 7,
            vmem=24,
            scratch=[
                pltpu.VMEM(value_cotangent.shape, bf16),
                pltpu.VMEM((4, side_rows, value_weight.shape[1]), bf16),
                pltpu.VMEM(value_weight.shape, bf16),
                pltpu.VMEM(value_weight.shape, bf16),
                pltpu.VMEM((6, tok_rows, down_part), bf16),
                pltpu.SemaphoreType.DMA((7,)),
                pltpu.SemaphoreType.DMA((6,)),
            ],
        )
        grad_input = call(
            place_kernel,
            shaped(tok_rows, width),
            pl.BlockSpec(memory_space=pl.ANY),
            at,
            z2,
            z3,
            grad_input,
            smem=1,
            specs=[VMEM, VMEM, pl.BlockSpec(memory_space=pl.ANY)],
            scratch=[pltpu.SemaphoreType.DMA((2,))],
            aliases={3: 0},
        )
        arrived, grad_input = lax.optimization_barrier((arrived, grad_input))
    grad_down, grad_up = call(
        total_kernel,
        (
            shaped(slots, rank, down_part, dtype=jnp.float32),
            shaped(slots, rank, up_part, dtype=jnp.float32),
        ),
        (VMEM, VMEM),
        want,
        count,
        arrived,
        smem=2,
    )
    if not by_permute:
        weight = lax.all_gather(value_weight, "fsdp", axis=0, tiled=True)
        adapter_term = jnp.concatenate(
            [
                jnp.dot(back, share[:, :down_part], preferred_element_type=jnp.float32)
                for share in factors
            ],
            axis=1,
        )
        frozen_term = jnp.einsum(
            "tc,dc->td", value_cotangent, weight, preferred_element_type=jnp.float32
        )
        grad_input = (frozen_term + adapter_term).astype(bf16)
    return (grad_input, grad_down, grad_up)


def solution(mesh):
    return jax.shard_map(
        per_device,
        mesh=mesh,
        in_specs=(
            P(("dp", "fsdp"), None),
            P(("dp", "fsdp"), None),
            P("fsdp", None),
            P("dp", None, "fsdp"),
            P("dp", None, "fsdp"),
            P(),
            P(),
        ),
        out_specs=(P(("dp", "fsdp"), None), P("dp", None, "fsdp"), P("dp", None, "fsdp")),
        check_vma=False,
    )
```

```python
import functools

import jax
import jax.numpy as jnp
from jax import lax
from jax.experimental import pallas as pl
from jax.experimental.pallas import tpu as pltpu
from jax.sharding import PartitionSpec as P

BLOCK = 128
LANES = 128
adapter_scale = 2.0

SMEM = pl.BlockSpec(memory_space=pltpu.SMEM)
VMEM = pl.BlockSpec(memory_space=pltpu.VMEM)
ANY = pl.BlockSpec(memory_space=pl.ANY)
NT = (((1,), (1,)), ((), ()))


def round_up(n):
    return -(-n // LANES) * LANES


def dot(a, b, dims=(((1,), (0,)), ((), ()))):
    return lax.dot_general(a, b, dims, preferred_element_type=jnp.float32)


def turned(a):
    return a.astype(jnp.float32).T.astype(a.dtype)


def fetch(sources, targets, sems):
    copies = [
        pltpu.make_async_copy(source, target, sems.at[i])
        for i, (source, target) in enumerate(zip(sources, targets))
    ]
    for copy in copies:
        copy.start()
    return copies


def copy_kernel(from_ref, to_ref, sem):
    copy = pltpu.make_async_copy(from_ref, to_ref, sem)
    copy.start()
    copy.wait()


def pick_kernel(
    group_blocks, me_ref, apb_hbm, row_hbm, down_hbm, up_hbm, w_hbm, send_ref, want_ref,
    count_ref, some_ref, apb_ref, row_ref, down_ref, up_ref, sems,
):
    rows = some_ref.shape[0]
    start = pl.multiple_of(lax.rem(me_ref[0], 2) * rows, 16)
    copies = fetch(
        (apb_hbm, row_hbm, down_hbm, up_hbm, w_hbm.at[pl.ds(start, rows)]),
        (
            apb_ref,
            row_ref,
            down_ref,
            up_ref,
            some_ref,
        ),
        sems,
    )
    slots, _, down_part = down_ref.shape
    up_part = up_ref.shape[2]
    up_at = round_up(down_part)
    groups = send_ref.shape[0]
    first = me_ref[0] * slots
    for s in range(slots):
        count_ref[s] = 0
    copies[0].wait()
    copies[1].wait()

    def group(g, carry):
        want_ref[g] = 0
        for j in range(group_blocks):
            local = row_ref[apb_ref[g * group_blocks + j]] - first

            @pl.when((local >= 0) & (local < slots))
            def _():
                want_ref[g] = local
                count_ref[local] = count_ref[local] + 1

        return carry

    lax.fori_loop(0, groups, group, 0)
    copies[2].wait()
    copies[3].wait()

    def put(g, carry):
        slot = want_ref[g]
        send_ref[g, :, :down_part] = down_ref[slot]
        send_ref[g, :, up_at : up_at + up_part] = up_ref[slot]
        return carry

    lax.fori_loop(0, groups, put, 0)
    copies[4].wait()


def peer_of(by_xor, at_ref, k):
    return lax.bitwise_xor(at_ref[0], k) if by_xor else k


def columns(ref, peer, width):
    if isinstance(peer, int):
        return ref[:, peer * width : (peer + 1) * width]
    return ref[:, pl.ds(pl.multiple_of(peer * width, LANES), width)]


def share_kernel(by_xor, slots, at_ref, me_ref, apb_ref, row_ref, got_ref, *out_refs):
    blocks = len(out_refs)
    for k, out_ref in enumerate(out_refs):
        block = me_ref[0] * blocks + peer_of(by_xor, at_ref, k)
        out_ref[...] = got_ref[lax.div(row_ref[apb_ref[block]], slots)]


def block_kernel(by_xor, down_part, up_part, shares, at_ref, x_ref, dy_ref, *refs):
    fac_refs, grads_refs, back_ref = refs[:shares], refs[shares:-1], refs[-1]
    up_at = round_up(down_part)
    wide = up_at + round_up(up_part)
    peers = [peer_of(by_xor, at_ref, k) for k in range(shares)]
    rank = fac_refs[0].shape[0]
    low_t = jnp.zeros((rank, BLOCK), jnp.float32)
    back_t = jnp.zeros((rank, BLOCK), jnp.float32)
    for k in range(shares):
        back_t += dot(
            fac_refs[k][:, up_at : up_at + up_part], columns(dy_ref, peers[k], up_part), NT
        )
    scaled = adapter_scale * back_t
    back = scaled.astype(jnp.bfloat16)
    back_ref[...] = scaled.T.astype(jnp.bfloat16)
    for k in range(shares):
        x = columns(x_ref, peers[k], down_part)
        low_t += dot(fac_refs[k][:, :down_part], x, NT)
        grads_refs[k][:, :down_part] = dot(back, x).astype(jnp.bfloat16)
        grads_refs[k][:, wide:] = back
    low = low_t.astype(jnp.bfloat16)
    for k in range(shares):
        grads_refs[k][:, up_at : up_at + up_part] = (
            adapter_scale * dot(low, columns(dy_ref, peers[k], up_part))
        ).astype(jnp.bfloat16)


def owner_kernel(by_xor, slots, at_ref, me_ref, apb_ref, row_ref, *refs):
    got_refs, out_ref, total_ref = refs[:-2], refs[-2], refs[-1]
    blocks = len(got_refs)
    wide = out_ref.shape[2]
    owners = [
        lax.div(row_ref[apb_ref[me_ref[0] * blocks + peer_of(by_xor, at_ref, k)]], slots)
        for k in range(blocks)
    ]
    out_ref[...] = jnp.zeros_like(out_ref)
    for j in range(blocks):
        total_ref[...] = got_refs[j][:, :wide].astype(jnp.float32)
        for i in range(blocks):
            if i != j:

                @pl.when(owners[i] == owners[j])
                def _():
                    total_ref[...] += got_refs[i][:, :wide].astype(jnp.float32)

        out_ref[owners[j]] = total_ref[...].astype(jnp.bfloat16)


def total_kernel(want_ref, count_ref, got_ref, down_ref, up_ref):
    slots, _, down_part = down_ref.shape
    up_part = up_ref.shape[2]
    up_at = round_up(down_part)
    down_ref[...] = jnp.zeros_like(down_ref)
    up_ref[...] = jnp.zeros_like(up_ref)

    def group(g, carry):
        slot = want_ref[g]
        down_ref[slot] += got_ref[g, :, :down_part].astype(jnp.float32)
        up_ref[slot] += got_ref[g, :, up_at : up_at + up_part].astype(jnp.float32)
        return carry

    lax.fori_loop(0, got_ref.shape[0], group, 0)
    for s in range(slots):
        divisor = jnp.maximum(count_ref[s], 1).astype(jnp.float32)
        down_ref[s] = down_ref[s] / divisor
        up_ref[s] = up_ref[s] / divisor


def far_kernel(near, w_hbm, dy_ref, share_ref, got_ref, z_ref, w_ref, sems):
    tokens, rows = z_ref.shape
    copies = fetch([w_hbm.at[pl.ds(near, rows)]], [w_ref], sems)
    dy_t = turned(dy_ref[...])
    back = turned(got_ref[:, got_ref.shape[1] - tokens :])
    adapted = dot(back, share_ref[:, near : near + rows])
    copies[0].wait()
    z_ref[...] = (dot(w_ref[...], dy_t).T + adapted).astype(jnp.bfloat16)


def input_kernel(
    at_ref, side_ref, back_ref, fac0_ref, fac1_ref, fac2_ref, fac3_ref, dy_hbm, y2_hbm, y3_hbm, x2_hbm, x3_hbm, w0_hbm, w1_hbm,
    out_ref, dy_ref, few_ref, w0_ref, w1_ref, buf, fetch_sems, sems,
):
    part = w0_ref.shape[0]
    fac_refs = (fac0_ref, fac1_ref, fac2_ref, fac3_ref)
    taken = few_ref.shape[1]
    side = side_ref[0] * taken
    few = [a.at[pl.ds(0, taken)] for a in (y2_hbm, y3_hbm, x2_hbm, x3_hbm)]
    fetches = fetch(
        (*few, w0_hbm, w1_hbm, dy_hbm),
        (*(few_ref.at[i] for i in range(4)), w0_ref, w1_ref, dy_ref),
        fetch_sems,
    )
    fetches[6].wait()
    dy_t = turned(dy_ref[...])
    copies = []
    for i, (k, w_ref, start, rows) in enumerate(
        (
            (2, few_ref.at[0], side, taken),
            (3, few_ref.at[1], side, taken),
            (2, few_ref.at[2], taken - side, taken),
            (3, few_ref.at[3], taken - side, taken),
            (0, w0_ref, 0, part),
            (1, w1_ref, 0, part),
        )
    ):
        fetches[i].wait()
        peer = lax.bitwise_xor(at_ref[0], k)
        start = pl.multiple_of(start, LANES)
        buf[i, :, :rows] = (
            dot(w_ref[...], dy_t).T
            + dot(back_ref[...], fac_refs[k][:, pl.ds(start, rows)])
        ).astype(jnp.bfloat16)
        first = pl.multiple_of(peer * part + start, LANES)
        copy = pltpu.make_async_copy(
            buf.at[i, :, pl.ds(0, rows)], out_ref.at[:, pl.ds(first, rows)], sems.at[i]
        )
        copy.start()
        copies.append(copy)
    for copy in copies:
        copy.wait()


def place_kernel(at_ref, z2_ref, z3_ref, in_ref, out_ref, sems):
    rows = z2_ref.shape[1]
    part = out_ref.shape[1] // 4
    copies = []
    for i, z_ref in enumerate((z2_ref, z3_ref)):
        peer = lax.bitwise_xor(at_ref[0], 2 + i)
        first = pl.multiple_of(peer * part + (part - rows), LANES)
        copy = pltpu.make_async_copy(z_ref, out_ref.at[:, pl.ds(first, rows)], sems.at[i])
        copy.start()
        copies.append(copy)
    for copy in copies:
        copy.wait()


def in_hbm(*arrays):
    return [pltpu.with_memory_space_constraint(a, pltpu.HBM) for a in arrays]


def call(
    kernel, out_shape, out_specs, *operands, smem=0, scratch=(), vmem=8, specs=None, aliases=None
):
    return pl.pallas_call(
        kernel,
        out_shape=out_shape,
        in_specs=[SMEM] * smem + (specs or [VMEM] * (len(operands) - smem)),
        input_output_aliases=aliases or {},
        out_specs=out_specs,
        scratch_shapes=scratch,
        compiler_params=pltpu.CompilerParams(vmem_limit_bytes=vmem << 20),
    )(*operands)


def per_device(
    projection_input,
    value_cotangent,
    value_weight,
    adapter_down_table,
    adapter_up_table,
    adapter_per_block,
    adapter_table_row,
):
    dp_count = lax.axis_size("dp")
    fsdp_count = lax.axis_size("fsdp")
    me = lax.axis_index("dp").reshape(1)
    at = lax.axis_index("fsdp")
    tok_rows, width = projection_input.shape
    slots, rank, down_part = adapter_down_table.shape
    up_part = adapter_up_table.shape[2]
    assert tok_rows == BLOCK
    wide = round_up(down_part) + round_up(up_part)
    bf16 = jnp.bfloat16

    def shaped(*shape, dtype=bf16):
        return jax.ShapeDtypeStruct(shape, dtype)

    by_permute = fsdp_count == 4 and down_part % 256 == 0
    by_permute = by_permute and dp_count % 2 == 0
    side_rows = round_up(down_part // 4) if by_permute else 16
    near_rows = 2 * side_rows

    def cross(array, bit, axis="fsdp"):
        return lax.ppermute(array, axis, [(i, i ^ bit) for i in range(lax.axis_size(axis))])

    def exchange(arrays):
        if by_permute:
            return [cross(a, k) if k else a for k, a in enumerate(arrays)]
        stacked = lax.all_to_all(jnp.stack(arrays), "fsdp", split_axis=0, concat_axis=0, tiled=True)
        return [stacked[k] for k in range(fsdp_count)]

    at = at.reshape(1)
    index = (me, adapter_per_block, adapter_table_row)
    send, want, count, some = call(
        functools.partial(pick_kernel, fsdp_count),
        (
            shaped(dp_count, rank, wide),
            shaped(dp_count, dtype=jnp.int32),
            shaped(slots, dtype=jnp.int32),
            shaped(side_rows, value_weight.shape[1]),
        ),
        (VMEM, SMEM, SMEM, VMEM),
        me,
        *in_hbm(*index[1:], adapter_down_table, adapter_up_table, value_weight),
        smem=1,
        specs=[ANY] * 5,
        scratch=[
            pltpu.SMEM(adapter_per_block.shape, jnp.int32),
            pltpu.SMEM(adapter_table_row.shape, jnp.int32),
            pltpu.VMEM(adapter_down_table.shape, bf16),
            pltpu.VMEM(adapter_up_table.shape, bf16),
            pltpu.SemaphoreType.DMA((5,)),
        ],
    )
    owned = lax.all_to_all(send, "dp", split_axis=0, concat_axis=0, tiled=True)
    if by_permute:
        side = me & 1
        y2 = cross(some, 2)
        dy2 = cross(value_cotangent, 2)
        at_hand, _ = lax.optimization_barrier((projection_input, send))
        at_hand = call(
            copy_kernel,
            shaped(tok_rows, width),
            VMEM,
            *in_hbm(at_hand),
            specs=[ANY],
            scratch=[pltpu.SemaphoreType.DMA],
        )
        owned, y2, at_hand = lax.optimization_barrier((owned, y2, at_hand))
    else:
        at_hand = projection_input
    share = call(
        functools.partial(share_kernel, by_permute, slots),
        [shaped(rank, wide)] * fsdp_count,
        [VMEM] * fsdp_count,
        at,
        *index,
        owned,
        smem=4,
    )
    if by_permute:
        x2, share, dy2 = lax.optimization_barrier((y2, share, dy2))
        x2 = cross(x2, 1, "dp")
    factors = exchange(share)
    *grads, back = call(
        functools.partial(block_kernel, by_permute, down_part, up_part, fsdp_count),
        [shaped(rank, wide + BLOCK)] * fsdp_count + [shaped(BLOCK, rank)],
        [VMEM] * (fsdp_count + 1),
        at,
        at_hand,
        value_cotangent,
        *factors,
        smem=1,
        vmem=20,
    )
    got = exchange(grads)
    if by_permute:
        got, dy2 = lax.optimization_barrier((got, dy2))
        dy3 = cross(dy2, 1)
    sums = call(
        functools.partial(owner_kernel, by_permute, slots),
        shaped(dp_count, rank, wide),
        VMEM,
        at,
        *index,
        *got,
        smem=4,
        scratch=[pltpu.VMEM((rank, wide), jnp.float32)],
    )
    if by_permute:
        sums, beside, y2, x2 = lax.optimization_barrier((sums, value_weight, y2, x2))
        near = cross(beside, 1), cross(y2, 1)
        x3 = cross(x2, 1)
    arrived = lax.all_to_all(sums, "dp", split_axis=0, concat_axis=0, tiled=True)
    if by_permute:
        far_rows = down_part - near_rows
        z2, z3 = (
            cross(
                call(
                    functools.partial(far_kernel, near_rows),
                    shaped(BLOCK, far_rows),
                    VMEM,
                    *in_hbm(value_weight),
                    dy,
                    share[bits],
                    got[bits],
                    specs=[ANY] + [VMEM] * 3,
                    vmem=12,
                    scratch=[
                        pltpu.VMEM((far_rows, value_weight.shape[1]), bf16),
                        pltpu.SemaphoreType.DMA((1,)),
                    ],
                ),
                bits,
            )
            for bits, dy in ((2, dy2), (3, dy3))
        )
        grad_input = call(
            input_kernel,
            shaped(tok_rows, width),
            pl.BlockSpec(memory_space=pl.ANY),
            at,
            side,
            back,
            *factors,
            *in_hbm(value_cotangent, y2),
            near[1],
            *in_hbm(x2),
            x3,
            *in_hbm(value_weight, near[0]),
            smem=2,
            specs=[VMEM] * 5 + [ANY] * 7,
            vmem=24,
            scratch=[
                pltpu.VMEM(value_cotangent.shape, bf16),
                pltpu.VMEM((4, side_rows, value_weight.shape[1]), bf16),
                pltpu.VMEM(value_weight.shape, bf16),
                pltpu.VMEM(value_weight.shape, bf16),
                pltpu.VMEM((6, tok_rows, down_part), bf16),
                pltpu.SemaphoreType.DMA((7,)),
                pltpu.SemaphoreType.DMA((6,)),
            ],
        )
        grad_input = call(
            place_kernel,
            shaped(tok_rows, width),
            pl.BlockSpec(memory_space=pl.ANY),
            at,
            z2,
            z3,
            grad_input,
            smem=1,
            specs=[VMEM, VMEM, pl.BlockSpec(memory_space=pl.ANY)],
            scratch=[pltpu.SemaphoreType.DMA((2,))],
            aliases={3: 0},
        )
        arrived, grad_input = lax.optimization_barrier((arrived, grad_input))
    grad_down, grad_up = call(
        total_kernel,
        (
            shaped(slots, rank, down_part, dtype=jnp.float32),
            shaped(slots, rank, up_part, dtype=jnp.float32),
        ),
        (VMEM, VMEM),
        want,
        count,
        arrived,
        smem=2,
    )
    if not by_permute:
        weight = lax.all_gather(value_weight, "fsdp", axis=0, tiled=True)
        adapter_term = jnp.concatenate(
            [
                jnp.dot(back, share[:, :down_part], preferred_element_type=jnp.float32)
                for share in factors
            ],
            axis=1,
        )
        frozen_term = jnp.einsum(
            "tc,dc->td", value_cotangent, weight, preferred_element_type=jnp.float32
        )
        grad_input = (frozen_term + adapter_term).astype(bf16)
    return (grad_input, grad_down, grad_up)


def solution(mesh):
    return jax.shard_map(
        per_device,
        mesh=mesh,
        in_specs=(
            P(("dp", "fsdp"), None),
            P(("dp", "fsdp"), None),
            P("fsdp", None),
            P("dp", None, "fsdp"),
            P("dp", None, "fsdp"),
            P(),
            P(),
        ),
        out_specs=(P(("dp", "fsdp"), None), P("dp", None, "fsdp"), P("dp", None, "fsdp")),
        check_vma=False,
    )
```

```python
import functools

import jax
import jax.numpy as jnp
from jax import lax
from jax.experimental import pallas as pl
from jax.experimental.pallas import tpu as pltpu
from jax.sharding import PartitionSpec as P

BLOCK = 128
LANES = 128
adapter_scale = 2.0

SMEM = pl.BlockSpec(memory_space=pltpu.SMEM)
VMEM = pl.BlockSpec(memory_space=pltpu.VMEM)
ANY = pl.BlockSpec(memory_space=pl.ANY)
NT = (((1,), (1,)), ((), ()))


def round_up(n):
    return -(-n // LANES) * LANES


def dot(a, b, dims=(((1,), (0,)), ((), ()))):
    return lax.dot_general(a, b, dims, preferred_element_type=jnp.float32)


def turned(a):
    return a.astype(jnp.float32).T.astype(a.dtype)


def fetch(sources, targets, sems):
    copies = [
        pltpu.make_async_copy(source, target, sems.at[i])
        for i, (source, target) in enumerate(zip(sources, targets))
    ]
    for copy in copies:
        copy.start()
    return copies


def early_kernel(x_hbm, w_hbm, dy_hbm, x_ref, own_hbm, w_ref, dy_ref, own_ref, sems):
    copies = fetch((dy_hbm, w_hbm, x_hbm), (dy_ref, w_ref, x_ref), sems)
    copies[0].wait()
    dy_t = turned(dy_ref[...])
    copies[1].wait()
    own_ref[...] = dot(w_ref[...], dy_t).T
    copies[2].wait()
    out = pltpu.make_async_copy(own_ref, own_hbm, sems.at[3])
    out.start()
    out.wait()


def pick_kernel(
    group_blocks, me_ref, apb_hbm, row_hbm, down_hbm, up_hbm, w_hbm, send_ref, want_ref,
    count_ref, some_ref, apb_ref, row_ref, down_ref, up_ref, sems,
):
    rows = some_ref.shape[0]
    start = pl.multiple_of(lax.rem(me_ref[0], 2) * rows, 16)
    copies = fetch(
        (apb_hbm, row_hbm, down_hbm, up_hbm, w_hbm.at[pl.ds(start, rows)]),
        (
            apb_ref,
            row_ref,
            down_ref,
            up_ref,
            some_ref,
        ),
        sems,
    )
    slots, _, down_part = down_ref.shape
    up_part = up_ref.shape[2]
    up_at = round_up(down_part)
    groups = send_ref.shape[0]
    first = me_ref[0] * slots
    for s in range(slots):
        count_ref[s] = 0
    copies[0].wait()
    copies[1].wait()

    def group(g, carry):
        want_ref[g] = 0
        for j in range(group_blocks):
            local = row_ref[apb_ref[g * group_blocks + j]] - first

            @pl.when((local >= 0) & (local < slots))
            def _():
                want_ref[g] = local
                count_ref[local] = count_ref[local] + 1

        return carry

    lax.fori_loop(0, groups, group, 0)
    copies[2].wait()
    copies[3].wait()

    def put(g, carry):
        slot = want_ref[g]
        send_ref[g, :, :down_part] = down_ref[slot]
        send_ref[g, :, up_at : up_at + up_part] = up_ref[slot]
        return carry

    lax.fori_loop(0, groups, put, 0)
    copies[4].wait()


def peer_of(by_xor, at_ref, k):
    return lax.bitwise_xor(at_ref[0], k) if by_xor else k


def columns(ref, peer, width):
    if isinstance(peer, int):
        return ref[:, peer * width : (peer + 1) * width]
    return ref[:, pl.ds(pl.multiple_of(peer * width, LANES), width)]


def share_kernel(by_xor, slots, at_ref, me_ref, apb_ref, row_ref, got_ref, *out_refs):
    blocks = len(out_refs)
    for k, out_ref in enumerate(out_refs):
        block = me_ref[0] * blocks + peer_of(by_xor, at_ref, k)
        out_ref[...] = got_ref[lax.div(row_ref[apb_ref[block]], slots)]


def block_kernel(by_xor, down_part, up_part, shares, at_ref, x_ref, dy_ref, *refs):
    fac_refs, grads_refs, back_ref = refs[:shares], refs[shares:-1], refs[-1]
    up_at = round_up(down_part)
    wide = up_at + round_up(up_part)
    peers = [peer_of(by_xor, at_ref, k) for k in range(shares)]
    rank = fac_refs[0].shape[0]
    low_t = jnp.zeros((rank, BLOCK), jnp.float32)
    back_t = jnp.zeros((rank, BLOCK), jnp.float32)
    for k in range(shares):
        back_t += dot(
            fac_refs[k][:, up_at : up_at + up_part], columns(dy_ref, peers[k], up_part), NT
        )
    scaled = adapter_scale * back_t
    back = scaled.astype(jnp.bfloat16)
    back_ref[...] = scaled.T.astype(jnp.bfloat16)
    for k in range(shares):
        x = columns(x_ref, peers[k], down_part)
        low_t += dot(fac_refs[k][:, :down_part], x, NT)
        grads_refs[k][:, :down_part] = dot(back, x).astype(jnp.bfloat16)
        grads_refs[k][:, wide:] = back
    low = low_t.astype(jnp.bfloat16)
    for k in range(shares):
        grads_refs[k][:, up_at : up_at + up_part] = (
            adapter_scale * dot(low, columns(dy_ref, peers[k], up_part))
        ).astype(jnp.bfloat16)


def owner_kernel(by_xor, slots, at_ref, me_ref, apb_ref, row_ref, *refs):
    got_refs, out_ref, total_ref = refs[:-2], refs[-2], refs[-1]
    blocks = len(got_refs)
    wide = out_ref.shape[2]
    owners = [
        lax.div(row_ref[apb_ref[me_ref[0] * blocks + peer_of(by_xor, at_ref, k)]], slots)
        for k in range(blocks)
    ]
    out_ref[...] = jnp.zeros_like(out_ref)
    for j in range(blocks):
        total_ref[...] = got_refs[j][:, :wide].astype(jnp.float32)
        for i in range(blocks):
            if i != j:

                @pl.when(owners[i] == owners[j])
                def _():
                    total_ref[...] += got_refs[i][:, :wide].astype(jnp.float32)

        out_ref[owners[j]] = total_ref[...].astype(jnp.bfloat16)


def total_kernel(want_ref, count_ref, got_ref, down_ref, up_ref):
    slots, _, down_part = down_ref.shape
    up_part = up_ref.shape[2]
    up_at = round_up(down_part)
    down_ref[...] = jnp.zeros_like(down_ref)
    up_ref[...] = jnp.zeros_like(up_ref)

    def group(g, carry):
        slot = want_ref[g]
        down_ref[slot] += got_ref[g, :, :down_part].astype(jnp.float32)
        up_ref[slot] += got_ref[g, :, up_at : up_at + up_part].astype(jnp.float32)
        return carry

    lax.fori_loop(0, got_ref.shape[0], group, 0)
    for s in range(slots):
        divisor = jnp.maximum(count_ref[s], 1).astype(jnp.float32)
        down_ref[s] = down_ref[s] / divisor
        up_ref[s] = up_ref[s] / divisor


def far_kernel(near, w_hbm, dy_ref, share_ref, got_ref, z_ref, w_ref, sems):
    tokens, rows = z_ref.shape
    copies = fetch([w_hbm.at[pl.ds(near, rows)]], [w_ref], sems)
    dy_t = turned(dy_ref[...])
    back = turned(got_ref[:, got_ref.shape[1] - tokens :])
    adapted = dot(back, share_ref[:, near : near + rows])
    copies[0].wait()
    z_ref[...] = (dot(w_ref[...], dy_t).T + adapted).astype(jnp.bfloat16)


def input_kernel(
    at_ref, side_ref, back_ref, fac0_ref, fac1_ref, fac2_ref, fac3_ref, dy_hbm, y2_hbm, y3_hbm, x2_hbm, x3_hbm, own_hbm, w1_hbm,
    out_ref, dy_ref, few_ref, own_ref, w1_ref, buf, fetch_sems, sems,
):
    part = w1_ref.shape[0]
    fac_refs = (fac0_ref, fac1_ref, fac2_ref, fac3_ref)
    taken = few_ref.shape[1]
    side = side_ref[0] * taken
    few = [a.at[pl.ds(0, taken)] for a in (y2_hbm, y3_hbm, x2_hbm, x3_hbm)]
    fetches = fetch(
        (*few, own_hbm, w1_hbm, dy_hbm),
        (*(few_ref.at[i] for i in range(4)), own_ref, w1_ref, dy_ref),
        fetch_sems,
    )
    fetches[6].wait()
    dy_t = turned(dy_ref[...])
    copies = []
    for i, (k, w_ref, start, rows) in enumerate(
        (
            (2, few_ref.at[0], side, taken),
            (3, few_ref.at[1], side, taken),
            (2, few_ref.at[2], taken - side, taken),
            (3, few_ref.at[3], taken - side, taken),
            (0, None, 0, part),
            (1, w1_ref, 0, part),
        )
    ):
        fetches[i].wait()
        peer = lax.bitwise_xor(at_ref[0], k)
        start = pl.multiple_of(start, LANES)
        buf[i, :, :rows] = (
            (dot(w_ref[...], dy_t).T if k else own_ref[...])
            + dot(back_ref[...], fac_refs[k][:, pl.ds(start, rows)])
        ).astype(jnp.bfloat16)
        first = pl.multiple_of(peer * part + start, LANES)
        copy = pltpu.make_async_copy(
            buf.at[i, :, pl.ds(0, rows)], out_ref.at[:, pl.ds(first, rows)], sems.at[i]
        )
        copy.start()
        copies.append(copy)
    for copy in copies:
        copy.wait()


def place_kernel(at_ref, z2_ref, z3_ref, in_ref, out_ref, sems):
    rows = z2_ref.shape[1]
    part = out_ref.shape[1] // 4
    copies = []
    for i, z_ref in enumerate((z2_ref, z3_ref)):
        peer = lax.bitwise_xor(at_ref[0], 2 + i)
        first = pl.multiple_of(peer * part + (part - rows), LANES)
        copy = pltpu.make_async_copy(z_ref, out_ref.at[:, pl.ds(first, rows)], sems.at[i])
        copy.start()
        copies.append(copy)
    for copy in copies:
        copy.wait()


def in_hbm(*arrays):
    return [pltpu.with_memory_space_constraint(a, pltpu.HBM) for a in arrays]


def call(
    kernel, out_shape, out_specs, *operands, smem=0, scratch=(), vmem=8, specs=None, aliases=None
):
    return pl.pallas_call(
        kernel,
        out_shape=out_shape,
        in_specs=[SMEM] * smem + (specs or [VMEM] * (len(operands) - smem)),
        input_output_aliases=aliases or {},
        out_specs=out_specs,
        scratch_shapes=scratch,
        compiler_params=pltpu.CompilerParams(vmem_limit_bytes=vmem << 20),
    )(*operands)


def per_device(
    projection_input,
    value_cotangent,
    value_weight,
    adapter_down_table,
    adapter_up_table,
    adapter_per_block,
    adapter_table_row,
):
    dp_count = lax.axis_size("dp")
    fsdp_count = lax.axis_size("fsdp")
    me = lax.axis_index("dp").reshape(1)
    at = lax.axis_index("fsdp")
    tok_rows, width = projection_input.shape
    slots, rank, down_part = adapter_down_table.shape
    up_part = adapter_up_table.shape[2]
    assert tok_rows == BLOCK
    wide = round_up(down_part) + round_up(up_part)
    bf16 = jnp.bfloat16

    def shaped(*shape, dtype=bf16):
        return jax.ShapeDtypeStruct(shape, dtype)

    by_permute = fsdp_count == 4 and down_part % 256 == 0
    by_permute = by_permute and dp_count % 2 == 0
    side_rows = round_up(down_part // 4) if by_permute else 16
    near_rows = 2 * side_rows

    def cross(array, bit, axis="fsdp"):
        return lax.ppermute(array, axis, [(i, i ^ bit) for i in range(lax.axis_size(axis))])

    def exchange(arrays):
        if by_permute:
            return [cross(a, k) if k else a for k, a in enumerate(arrays)]
        stacked = lax.all_to_all(jnp.stack(arrays), "fsdp", split_axis=0, concat_axis=0, tiled=True)
        return [stacked[k] for k in range(fsdp_count)]

    at = at.reshape(1)
    index = (me, adapter_per_block, adapter_table_row)
    send, want, count, some = call(
        functools.partial(pick_kernel, fsdp_count),
        (
            shaped(dp_count, rank, wide),
            shaped(dp_count, dtype=jnp.int32),
            shaped(slots, dtype=jnp.int32),
            shaped(side_rows, value_weight.shape[1]),
        ),
        (VMEM, SMEM, SMEM, VMEM),
        me,
        *in_hbm(*index[1:], adapter_down_table, adapter_up_table, value_weight),
        smem=1,
        specs=[ANY] * 5,
        scratch=[
            pltpu.SMEM(adapter_per_block.shape, jnp.int32),
            pltpu.SMEM(adapter_table_row.shape, jnp.int32),
            pltpu.VMEM(adapter_down_table.shape, bf16),
            pltpu.VMEM(adapter_up_table.shape, bf16),
            pltpu.SemaphoreType.DMA((5,)),
        ],
    )
    owned = lax.all_to_all(send, "dp", split_axis=0, concat_axis=0, tiled=True)
    if by_permute:
        side = me & 1
        y2 = cross(some, 2)
        dy2 = cross(value_cotangent, 2)
        at_hand, _ = lax.optimization_barrier((projection_input, send))
        at_hand, own = call(
            early_kernel,
            (shaped(tok_rows, width), shaped(tok_rows, down_part, dtype=jnp.float32)),
            (VMEM, ANY),
            *in_hbm(at_hand, value_weight, value_cotangent),
            specs=[ANY] * 3,
            vmem=16,
            scratch=[
                pltpu.VMEM(value_weight.shape, bf16),
                pltpu.VMEM(value_cotangent.shape, bf16),
                pltpu.VMEM((tok_rows, down_part), jnp.float32),
                pltpu.SemaphoreType.DMA((4,)),
            ],
        )
        owned, y2, at_hand, own = lax.optimization_barrier((owned, y2, at_hand, own))
    else:
        at_hand = projection_input
    share = call(
        functools.partial(share_kernel, by_permute, slots),
        [shaped(rank, wide)] * fsdp_count,
        [VMEM] * fsdp_count,
        at,
        *index,
        owned,
        smem=4,
    )
    if by_permute:
        x2 = y2
        x2 = cross(x2, 1, "dp")
    factors = exchange(share)
    if by_permute:
        factors, dy2 = lax.optimization_barrier((factors, dy2))
    *grads, back = call(
        functools.partial(block_kernel, by_permute, down_part, up_part, fsdp_count),
        [shaped(rank, wide + BLOCK)] * fsdp_count + [shaped(BLOCK, rank)],
        [VMEM] * (fsdp_count + 1),
        at,
        at_hand,
        value_cotangent,
        *factors,
        smem=1,
        vmem=20,
    )
    got = exchange(grads)
    if by_permute:
        got, dy2 = lax.optimization_barrier((got, dy2))
        dy3 = cross(dy2, 1)
    sums = call(
        functools.partial(owner_kernel, by_permute, slots),
        shaped(dp_count, rank, wide),
        VMEM,
        at,
        *index,
        *got,
        smem=4,
        scratch=[pltpu.VMEM((rank, wide), jnp.float32)],
    )
    if by_permute:
        sums, beside, y2, x2 = lax.optimization_barrier((sums, value_weight, y2, x2))
        near = cross(beside, 1), cross(y2, 1)
        x3 = cross(x2, 1)
    arrived = lax.all_to_all(sums, "dp", split_axis=0, concat_axis=0, tiled=True)
    if by_permute:
        far_rows = down_part - near_rows
        z2, z3 = (
            cross(
                call(
                    functools.partial(far_kernel, near_rows),
                    shaped(BLOCK, far_rows),
                    VMEM,
                    *in_hbm(value_weight),
                    dy,
                    share[bits],
                    got[bits],
                    specs=[ANY] + [VMEM] * 3,
                    vmem=12,
                    scratch=[
                        pltpu.VMEM((far_rows, value_weight.shape[1]), bf16),
                        pltpu.SemaphoreType.DMA((1,)),
                    ],
                ),
                bits,
            )
            for bits, dy in ((2, dy2), (3, dy3))
        )
        grad_input = call(
            input_kernel,
            shaped(tok_rows, width),
            pl.BlockSpec(memory_space=pl.ANY),
            at,
            side,
            back,
            *factors,
            *in_hbm(value_cotangent, y2),
            near[1],
            *in_hbm(x2),
            x3,
            *in_hbm(own, near[0]),
            smem=2,
            specs=[VMEM] * 5 + [ANY] * 7,
            vmem=24,
            scratch=[
                pltpu.VMEM(value_cotangent.shape, bf16),
                pltpu.VMEM((4, side_rows, value_weight.shape[1]), bf16),
                pltpu.VMEM((tok_rows, down_part), jnp.float32),
                pltpu.VMEM(value_weight.shape, bf16),
                pltpu.VMEM((6, tok_rows, down_part), bf16),
                pltpu.SemaphoreType.DMA((7,)),
                pltpu.SemaphoreType.DMA((6,)),
            ],
        )
        grad_input = call(
            place_kernel,
            shaped(tok_rows, width),
            pl.BlockSpec(memory_space=pl.ANY),
            at,
            z2,
            z3,
            grad_input,
            smem=1,
            specs=[VMEM, VMEM, pl.BlockSpec(memory_space=pl.ANY)],
            scratch=[pltpu.SemaphoreType.DMA((2,))],
            aliases={3: 0},
        )
        arrived, grad_input = lax.optimization_barrier((arrived, grad_input))
    grad_down, grad_up = call(
        total_kernel,
        (
            shaped(slots, rank, down_part, dtype=jnp.float32),
            shaped(slots, rank, up_part, dtype=jnp.float32),
        ),
        (VMEM, VMEM),
        want,
        count,
        arrived,
        smem=2,
    )
    if not by_permute:
        weight = lax.all_gather(value_weight, "fsdp", axis=0, tiled=True)
        adapter_term = jnp.concatenate(
            [
                jnp.dot(back, share[:, :down_part], preferred_element_type=jnp.float32)
                for share in factors
            ],
            axis=1,
        )
        frozen_term = jnp.einsum(
            "tc,dc->td", value_cotangent, weight, preferred_element_type=jnp.float32
        )
        grad_input = (frozen_term + adapter_term).astype(bf16)
    return (grad_input, grad_down, grad_up)


def solution(mesh):
    return jax.shard_map(
        per_device,
        mesh=mesh,
        in_specs=(
            P(("dp", "fsdp"), None),
            P(("dp", "fsdp"), None),
            P("fsdp", None),
            P("dp", None, "fsdp"),
            P("dp", None, "fsdp"),
            P(),
            P(),
        ),
        out_specs=(P(("dp", "fsdp"), None), P("dp", None, "fsdp"), P("dp", None, "fsdp")),
        check_vma=False,
    )
```

```python
import functools

import jax
import jax.numpy as jnp
from jax import lax
from jax.experimental import pallas as pl
from jax.experimental.pallas import tpu as pltpu
from jax.sharding import PartitionSpec as P

BLOCK = 128
LANES = 128
adapter_scale = 2.0

SMEM = pl.BlockSpec(memory_space=pltpu.SMEM)
VMEM = pl.BlockSpec(memory_space=pltpu.VMEM)
ANY = pl.BlockSpec(memory_space=pl.ANY)
NT = (((1,), (1,)), ((), ()))


def round_up(n):
    return -(-n // LANES) * LANES


def dot(a, b, dims=(((1,), (0,)), ((), ()))):
    return lax.dot_general(a, b, dims, preferred_element_type=jnp.float32)


def turned(a):
    return a.astype(jnp.float32).T.astype(a.dtype)


def fetch(sources, targets, sems):
    copies = [
        pltpu.make_async_copy(source, target, sems.at[i])
        for i, (source, target) in enumerate(zip(sources, targets))
    ]
    for copy in copies:
        copy.start()
    return copies


def early_kernel(x_hbm, w_hbm, dy_hbm, x_ref, own_hbm, w_ref, dy_ref, own_ref, sems):
    copies = fetch((dy_hbm, w_hbm, x_hbm), (dy_ref, w_ref, x_ref), sems)
    copies[0].wait()
    dy_t = turned(dy_ref[...])
    copies[1].wait()
    own_ref[...] = dot(w_ref[...], dy_t).T
    copies[2].wait()
    out = pltpu.make_async_copy(own_ref, own_hbm, sems.at[3])
    out.start()
    out.wait()


def pick_kernel(
    group_blocks, me_ref, apb_hbm, row_hbm, down_hbm, up_hbm, w_hbm, send_ref, want_ref,
    count_ref, some_ref, apb_ref, row_ref, down_ref, up_ref, sems,
):
    rows = some_ref.shape[0]
    start = pl.multiple_of(lax.rem(me_ref[0], 2) * rows, 16)
    copies = fetch(
        (apb_hbm, row_hbm, down_hbm, up_hbm, w_hbm.at[pl.ds(start, rows)]),
        (
            apb_ref,
            row_ref,
            down_ref,
            up_ref,
            some_ref,
        ),
        sems,
    )
    slots, _, down_part = down_ref.shape
    up_part = up_ref.shape[2]
    up_at = round_up(down_part)
    groups = send_ref.shape[0]
    first = me_ref[0] * slots
    for s in range(slots):
        count_ref[s] = 0
    copies[0].wait()
    copies[1].wait()

    def group(g, carry):
        want = jnp.int32(0)
        for j in range(group_blocks):
            local = row_ref[apb_ref[g * group_blocks + j]] - first
            mine = (local >= 0) & (local < slots)
            want = jnp.where(mine, local, want)
            slot = jnp.where(mine, local, 0)
            count_ref[slot] = count_ref[slot] + mine.astype(jnp.int32)
        want_ref[g] = want
        return carry

    lax.fori_loop(0, groups, group, 0, unroll=4)
    copies[2].wait()
    copies[3].wait()

    def put(g, carry):
        slot = want_ref[g]
        send_ref[g, :, :down_part] = down_ref[slot]
        send_ref[g, :, up_at : up_at + up_part] = up_ref[slot]
        return carry

    lax.fori_loop(0, groups, put, 0)
    copies[4].wait()


def peer_of(by_xor, at_ref, k):
    return lax.bitwise_xor(at_ref[0], k) if by_xor else k


def columns(ref, peer, width):
    if isinstance(peer, int):
        return ref[:, peer * width : (peer + 1) * width]
    return ref[:, pl.ds(pl.multiple_of(peer * width, LANES), width)]


def share_kernel(by_xor, slots, at_ref, me_ref, apb_ref, row_ref, got_ref, *out_refs):
    blocks = len(out_refs)
    for k, out_ref in enumerate(out_refs):
        block = me_ref[0] * blocks + peer_of(by_xor, at_ref, k)
        out_ref[...] = got_ref[lax.div(row_ref[apb_ref[block]], slots)]


def block_kernel(by_xor, down_part, up_part, shares, at_ref, x_ref, dy_ref, *refs):
    fac_refs, grads_refs, back_ref = refs[:shares], refs[shares:-1], refs[-1]
    up_at = round_up(down_part)
    wide = up_at + round_up(up_part)
    peers = [peer_of(by_xor, at_ref, k) for k in range(shares)]
    rank = fac_refs[0].shape[0]
    low_t = jnp.zeros((rank, BLOCK), jnp.float32)
    back_t = jnp.zeros((rank, BLOCK), jnp.float32)
    for k in range(shares):
        back_t += dot(
            fac_refs[k][:, up_at : up_at + up_part], columns(dy_ref, peers[k], up_part), NT
        )
    scaled = adapter_scale * back_t
    back = scaled.astype(jnp.bfloat16)
    back_ref[...] = scaled.T.astype(jnp.bfloat16)
    for k in range(shares):
        x = columns(x_ref, peers[k], down_part)
        low_t += dot(fac_refs[k][:, :down_part], x, NT)
        grads_refs[k][:, :down_part] = dot(back, x).astype(jnp.bfloat16)
        grads_refs[k][:, wide:] = back
    low = low_t.astype(jnp.bfloat16)
    for k in range(shares):
        grads_refs[k][:, up_at : up_at + up_part] = (
            adapter_scale * dot(low, columns(dy_ref, peers[k], up_part))
        ).astype(jnp.bfloat16)


def owner_kernel(by_xor, slots, at_ref, me_ref, apb_ref, row_ref, *refs):
    got_refs, out_ref, total_ref = refs[:-2], refs[-2], refs[-1]
    blocks = len(got_refs)
    wide = out_ref.shape[2]
    owners = [
        lax.div(row_ref[apb_ref[me_ref[0] * blocks + peer_of(by_xor, at_ref, k)]], slots)
        for k in range(blocks)
    ]
    out_ref[...] = jnp.zeros_like(out_ref)
    for j in range(blocks):
        total_ref[...] = got_refs[j][:, :wide].astype(jnp.float32)
        for i in range(blocks):
            if i != j:

                @pl.when(owners[i] == owners[j])
                def _():
                    total_ref[...] += got_refs[i][:, :wide].astype(jnp.float32)

        out_ref[owners[j]] = total_ref[...].astype(jnp.bfloat16)


def total_kernel(want_ref, count_ref, got_ref, down_ref, up_ref):
    slots, _, down_part = down_ref.shape
    up_part = up_ref.shape[2]
    up_at = round_up(down_part)
    down_ref[...] = jnp.zeros_like(down_ref)
    up_ref[...] = jnp.zeros_like(up_ref)

    def group(g, carry):
        slot = want_ref[g]
        down_ref[slot] += got_ref[g, :, :down_part].astype(jnp.float32)
        up_ref[slot] += got_ref[g, :, up_at : up_at + up_part].astype(jnp.float32)
        return carry

    lax.fori_loop(0, got_ref.shape[0], group, 0)
    for s in range(slots):
        divisor = jnp.maximum(count_ref[s], 1).astype(jnp.float32)
        down_ref[s] = down_ref[s] / divisor
        up_ref[s] = up_ref[s] / divisor


def far_kernel(near, w_hbm, dy_ref, share_ref, got_ref, z_ref, w_ref, sems):
    tokens, rows = z_ref.shape
    copies = fetch([w_hbm.at[pl.ds(near, rows)]], [w_ref], sems)
    dy_t = turned(dy_ref[...])
    back = turned(got_ref[:, got_ref.shape[1] - tokens :])
    adapted = dot(back, share_ref[:, near : near + rows])
    copies[0].wait()
    z_ref[...] = (dot(w_ref[...], dy_t).T + adapted).astype(jnp.bfloat16)


def input_kernel(
    at_ref, side_ref, back_ref, fac0_ref, fac1_ref, fac2_ref, fac3_ref, dy_hbm, y2_hbm, y3_hbm, x2_hbm, x3_hbm, own_hbm, w1_hbm,
    out_ref, dy_ref, few_ref, own_ref, w1_ref, buf, fetch_sems, sems,
):
    part = w1_ref.shape[0]
    fac_refs = (fac0_ref, fac1_ref, fac2_ref, fac3_ref)
    taken = few_ref.shape[1]
    side = side_ref[0] * taken
    few = [a.at[pl.ds(0, taken)] for a in (y2_hbm, y3_hbm, x2_hbm, x3_hbm)]
    fetches = fetch(
        (*few, own_hbm, w1_hbm, dy_hbm),
        (*(few_ref.at[i] for i in range(4)), own_ref, w1_ref, dy_ref),
        fetch_sems,
    )
    fetches[6].wait()
    dy_t = turned(dy_ref[...])
    copies = []
    for i, (k, w_ref, start, rows) in enumerate(
        (
            (2, few_ref.at[0], side, taken),
            (3, few_ref.at[1], side, taken),
            (2, few_ref.at[2], taken - side, taken),
            (3, few_ref.at[3], taken - side, taken),
            (0, None, 0, part),
            (1, w1_ref, 0, part),
        )
    ):
        fetches[i].wait()
        peer = lax.bitwise_xor(at_ref[0], k)
        start = pl.multiple_of(start, LANES)
        buf[i, :, :rows] = (
            (dot(w_ref[...], dy_t).T if k else own_ref[...])
            + dot(back_ref[...], fac_refs[k][:, pl.ds(start, rows)])
        ).astype(jnp.bfloat16)
        first = pl.multiple_of(peer * part + start, LANES)
        copy = pltpu.make_async_copy(
            buf.at[i, :, pl.ds(0, rows)], out_ref.at[:, pl.ds(first, rows)], sems.at[i]
        )
        copy.start()
        copies.append(copy)
    for copy in copies:
        copy.wait()


def last_kernel(
    want_ref, count_ref, at_ref, got_ref, z2_ref, z3_ref, in_ref, down_ref, up_ref, out_ref, sems
):
    rows = z2_ref.shape[1]
    part = out_ref.shape[1] // 4
    copies = []
    for i, z_ref in enumerate((z2_ref, z3_ref)):
        peer = lax.bitwise_xor(at_ref[0], 2 + i)
        first = pl.multiple_of(peer * part + (part - rows), LANES)
        copy = pltpu.make_async_copy(z_ref, out_ref.at[:, pl.ds(first, rows)], sems.at[i])
        copy.start()
        copies.append(copy)
    total_kernel(want_ref, count_ref, got_ref, down_ref, up_ref)
    for copy in copies:
        copy.wait()


def in_hbm(*arrays):
    return [pltpu.with_memory_space_constraint(a, pltpu.HBM) for a in arrays]


def call(
    kernel, out_shape, out_specs, *operands, smem=0, scratch=(), vmem=8, specs=None, aliases=None
):
    return pl.pallas_call(
        kernel,
        out_shape=out_shape,
        in_specs=[SMEM] * smem + (specs or [VMEM] * (len(operands) - smem)),
        input_output_aliases=aliases or {},
        out_specs=out_specs,
        scratch_shapes=scratch,
        compiler_params=pltpu.CompilerParams(vmem_limit_bytes=vmem << 20),
    )(*operands)


def per_device(
    projection_input,
    value_cotangent,
    value_weight,
    adapter_down_table,
    adapter_up_table,
    adapter_per_block,
    adapter_table_row,
):
    dp_count = lax.axis_size("dp")
    fsdp_count = lax.axis_size("fsdp")
    me = lax.axis_index("dp").reshape(1)
    at = lax.axis_index("fsdp")
    tok_rows, width = projection_input.shape
    slots, rank, down_part = adapter_down_table.shape
    up_part = adapter_up_table.shape[2]
    assert tok_rows == BLOCK
    wide = round_up(down_part) + round_up(up_part)
    bf16 = jnp.bfloat16

    def shaped(*shape, dtype=bf16):
        return jax.ShapeDtypeStruct(shape, dtype)

    by_permute = fsdp_count == 4 and down_part % 256 == 0
    by_permute = by_permute and dp_count % 2 == 0
    side_rows = round_up(down_part // 4) if by_permute else 16
    near_rows = 2 * side_rows

    def cross(array, bit, axis="fsdp"):
        return lax.ppermute(array, axis, [(i, i ^ bit) for i in range(lax.axis_size(axis))])

    def exchange(arrays):
        if by_permute:
            return [cross(a, k) if k else a for k, a in enumerate(arrays)]
        stacked = lax.all_to_all(jnp.stack(arrays), "fsdp", split_axis=0, concat_axis=0, tiled=True)
        return [stacked[k] for k in range(fsdp_count)]

    at = at.reshape(1)
    index = (me, adapter_per_block, adapter_table_row)
    send, want, count, some = call(
        functools.partial(pick_kernel, fsdp_count),
        (
            shaped(dp_count, rank, wide),
            shaped(dp_count, dtype=jnp.int32),
            shaped(slots, dtype=jnp.int32),
            shaped(side_rows, value_weight.shape[1]),
        ),
        (VMEM, SMEM, SMEM, VMEM),
        me,
        *in_hbm(*index[1:], adapter_down_table, adapter_up_table, value_weight),
        smem=1,
        specs=[ANY] * 5,
        scratch=[
            pltpu.SMEM(adapter_per_block.shape, jnp.int32),
            pltpu.SMEM(adapter_table_row.shape, jnp.int32),
            pltpu.VMEM(adapter_down_table.shape, bf16),
            pltpu.VMEM(adapter_up_table.shape, bf16),
            pltpu.SemaphoreType.DMA((5,)),
        ],
    )
    owned = lax.all_to_all(send, "dp", split_axis=0, concat_axis=0, tiled=True)
    if by_permute:
        side = me & 1
        y2 = cross(some, 2)
        dy2 = cross(value_cotangent, 2)
        at_hand, _ = lax.optimization_barrier((projection_input, send))
        at_hand, own = call(
            early_kernel,
            (shaped(tok_rows, width), shaped(tok_rows, down_part, dtype=jnp.float32)),
            (VMEM, ANY),
            *in_hbm(at_hand, value_weight, value_cotangent),
            specs=[ANY] * 3,
            vmem=16,
            scratch=[
                pltpu.VMEM(value_weight.shape, bf16),
                pltpu.VMEM(value_cotangent.shape, bf16),
                pltpu.VMEM((tok_rows, down_part), jnp.float32),
                pltpu.SemaphoreType.DMA((4,)),
            ],
        )
        owned, y2, at_hand, own = lax.optimization_barrier((owned, y2, at_hand, own))
    else:
        at_hand = projection_input
    share = call(
        functools.partial(share_kernel, by_permute, slots),
        [shaped(rank, wide)] * fsdp_count,
        [VMEM] * fsdp_count,
        at,
        *index,
        owned,
        smem=4,
    )
    if by_permute:
        x2 = y2
        x2 = cross(x2, 1, "dp")
    factors = exchange(share)
    if by_permute:
        factors, dy2 = lax.optimization_barrier((factors, dy2))
    *grads, back = call(
        functools.partial(block_kernel, by_permute, down_part, up_part, fsdp_count),
        [shaped(rank, wide + BLOCK)] * fsdp_count + [shaped(BLOCK, rank)],
        [VMEM] * (fsdp_count + 1),
        at,
        at_hand,
        value_cotangent,
        *factors,
        smem=1,
        vmem=20,
    )
    got = exchange(grads)
    if by_permute:
        got, dy2 = lax.optimization_barrier((got, dy2))
        dy3 = cross(dy2, 1)
    sums = call(
        functools.partial(owner_kernel, by_permute, slots),
        shaped(dp_count, rank, wide),
        VMEM,
        at,
        *index,
        *got,
        smem=4,
        scratch=[pltpu.VMEM((rank, wide), jnp.float32)],
    )
    if by_permute:
        sums, beside, y2, x2 = lax.optimization_barrier((sums, value_weight, y2, x2))
        near = cross(beside, 1), cross(y2, 1)
        x3 = cross(x2, 1)
    arrived = lax.all_to_all(sums, "dp", split_axis=0, concat_axis=0, tiled=True)
    if by_permute:
        far_rows = down_part - near_rows
        z2, z3 = (
            cross(
                call(
                    functools.partial(far_kernel, near_rows),
                    shaped(BLOCK, far_rows),
                    VMEM,
                    *in_hbm(value_weight),
                    dy,
                    share[bits],
                    got[bits],
                    specs=[ANY] + [VMEM] * 3,
                    vmem=12,
                    scratch=[
                        pltpu.VMEM((far_rows, value_weight.shape[1]), bf16),
                        pltpu.SemaphoreType.DMA((1,)),
                    ],
                ),
                bits,
            )
            for bits, dy in ((2, dy2), (3, dy3))
        )
        grad_input = call(
            input_kernel,
            shaped(tok_rows, width),
            pl.BlockSpec(memory_space=pl.ANY),
            at,
            side,
            back,
            *factors,
            *in_hbm(value_cotangent, y2),
            near[1],
            *in_hbm(x2),
            x3,
            *in_hbm(own, near[0]),
            smem=2,
            specs=[VMEM] * 5 + [ANY] * 7,
            vmem=24,
            scratch=[
                pltpu.VMEM(value_cotangent.shape, bf16),
                pltpu.VMEM((4, side_rows, value_weight.shape[1]), bf16),
                pltpu.VMEM((tok_rows, down_part), jnp.float32),
                pltpu.VMEM(value_weight.shape, bf16),
                pltpu.VMEM((6, tok_rows, down_part), bf16),
                pltpu.SemaphoreType.DMA((7,)),
                pltpu.SemaphoreType.DMA((6,)),
            ],
        )
        grad_down, grad_up, grad_input = call(
            last_kernel,
            (
                shaped(slots, rank, down_part, dtype=jnp.float32),
                shaped(slots, rank, up_part, dtype=jnp.float32),
                shaped(tok_rows, width),
            ),
            (VMEM, VMEM, ANY),
            want,
            count,
            at,
            arrived,
            z2,
            z3,
            grad_input,
            smem=3,
            specs=[VMEM, VMEM, VMEM, ANY],
            scratch=[pltpu.SemaphoreType.DMA((2,))],
            aliases={6: 2},
        )
    else:
        grad_down, grad_up = call(
            total_kernel,
            (
                shaped(slots, rank, down_part, dtype=jnp.float32),
                shaped(slots, rank, up_part, dtype=jnp.float32),
            ),
            (VMEM, VMEM),
            want,
            count,
            arrived,
            smem=2,
        )
        weight = lax.all_gather(value_weight, "fsdp", axis=0, tiled=True)
        adapter_term = jnp.concatenate(
            [
                jnp.dot(back, share[:, :down_part], preferred_element_type=jnp.float32)
                for share in factors
            ],
            axis=1,
        )
        frozen_term = jnp.einsum(
            "tc,dc->td", value_cotangent, weight, preferred_element_type=jnp.float32
        )
        grad_input = (frozen_term + adapter_term).astype(bf16)
    return (grad_input, grad_down, grad_up)


def solution(mesh):
    return jax.shard_map(
        per_device,
        mesh=mesh,
        in_specs=(
            P(("dp", "fsdp"), None),
            P(("dp", "fsdp"), None),
            P("fsdp", None),
            P("dp", None, "fsdp"),
            P("dp", None, "fsdp"),
            P(),
            P(),
        ),
        out_specs=(P(("dp", "fsdp"), None), P("dp", None, "fsdp"), P("dp", None, "fsdp")),
        check_vma=False,
    )
```
